32 devices in a mesh: ctx: 8 (over y, x, core), head: 4 (over z).
Axes of the slice: x: 2, y: 2, z: 4, core: 2. Of those that a mesh axis runs over, the one named last changes fastest.
Arguments:
- hidden_in: bfloat16 [1024, 4096], P('ctx', 'head'), may hold values from -6 to 6
- queries: bfloat16 [1024, 4096], P('ctx', 'head'), may hold values from -16 to 16
- kv_prev: bfloat16 [1024, 2, 4096], P('ctx', None, 'head'), may hold values from -16 to 16
- norm_gain: bfloat16 [4096], replicated, may hold values from 0.099609375 to 1.8984375
- w_kv: bfloat16 [4096, 2, 4096], P(None, None, 'head'), may hold values from -0.09375 to 0.09375
- w_out: bfloat16 [4096, 4096], P('head', 'ctx'), may hold values from -0.1875 to 0.1875
Outputs:
- hidden_out: float32 [1024, 4096], P('ctx', 'head')
- kv_out: float32 [1024, 2, 4096], P('ctx', None, 'head')
The draws below stay inside these ranges and needn't reach their ends.
All inputs are finite; a program needn't handle non-finite values.
Results may differ from the reference program's by a relative error of at most 0.033.
Values may be sent and summed in bfloat16 or wider, within the bound.
A program may use at most 128 MiB of HBM per device.

```python
import jax
import jax.numpy as jnp
from jax import lax

D = 4096
HEADS = 32
HD = 128
ITERS = 2
SEQ = 1024
N_HEAD = 4


def shared_pair(key):
    folded = jax.random.fold_in(key, 1931)
    key_query, key_keys, key_values = jax.random.split(folded, 3)
    query_draw = jnp.clip(jax.random.normal(key_query, (SEQ, D), jnp.float32), -4.0, 4.0)
    key_draw = jnp.clip(jax.random.normal(key_keys, (SEQ, D), jnp.float32), -4.0, 4.0)
    value_draw = jnp.clip(jax.random.normal(key_values, (SEQ, D), jnp.float32), -4.0, 4.0)
    return (query_draw, jnp.stack([key_draw, value_draw], axis=1))


def draw_queries(key, part):
    return shared_pair(key)[0].astype(jnp.bfloat16)


def draw_kv_prev(key, part):
    return shared_pair(key)[1].astype(jnp.bfloat16)


def draw_hidden_in(key, part):
    key_first, key_second = jax.random.split(jax.random.fold_in(key, 577))
    columns = jnp.arange(D).astype(jnp.float32) / D
    drawn = jnp.clip(jax.random.normal(key_first, (SEQ, D), jnp.float32), -4.0, 4.0)
    drawn = drawn * jax.random.uniform(key_second, (SEQ, D), jnp.float32, 0.6, 1.4)
    rising = 0.25 * jnp.exp(jnp.log(3.0) * columns)
    return (drawn * rising[None, :]).astype(jnp.bfloat16)


def block_scale(own_key, dims, pieces, smallest, top_value):
    def one(dim, parts):
        steps = jax.random.uniform(jax.random.fold_in(jax.random.fold_in(own_key, 6), dim), (parts,), jnp.float32, smallest / len(pieces), top_value / len(pieces))
        return jnp.repeat(jnp.exp(steps), dims[dim] // parts).reshape((-1,) + (1,) * (len(dims) - dim - 1))

    loudness = one(*pieces[0])
    for cut in pieces[1:]:
        loudness = loudness * one(*cut)
    return loudness


def scatter_about(stream_key, shape, scale, reach, cuts=(), held_as=jnp.bfloat16):
    gain = block_scale(stream_key, shape, cuts, -0.22, 0.18) if cuts else 1.0
    result = jax.random.normal(stream_key, shape, jnp.float32) * scale * gain
    return jnp.minimum(jnp.maximum(result, -reach), reach).astype(held_as)


def setup_inputs(seed: int = 0) -> dict:
    arg_keys = jax.random.split(jax.random.key(seed), 7)
    hidden_in = draw_hidden_in(jax.random.fold_in(arg_keys[6], 71), 0)
    queries = draw_queries(jax.random.fold_in(arg_keys[6], 71), 0)
    kv_prev = draw_kv_prev(jax.random.fold_in(arg_keys[6], 71), 0)
    norm_gain = jnp.clip(1.0 + 0.18 * jax.random.normal(arg_keys[3], (D,), jnp.float32), 0.099609375, 1.8984375).astype(jnp.bfloat16)
    w_kv = scatter_about(arg_keys[4], (D, 2, D), D ** -0.5, 0.09375, ((2, 4),))
    w_out = scatter_about(arg_keys[5], (D, D), (D // 4) ** -0.5, 0.1875, ((0, 4), (1, 8)))
    return dict(hidden_in=hidden_in, queries=queries, kv_prev=kv_prev, norm_gain=norm_gain, w_kv=w_kv, w_out=w_out)


MASKED = -1e+30
EPSILON = 1e-05

def attend_head(triple):
    query_rows, key_rows, value_rows = triple
    scores = jnp.dot(query_rows, key_rows.T, preferred_element_type=jnp.float32) * HD ** (-0.5)
    positions = jnp.arange(query_rows.shape[0])
    causal = positions[:, None] >= positions[None, :]
    scores = jnp.where(causal, scores, MASKED)
    row_max = lax.optimization_barrier(jnp.max(scores, axis=1, keepdims=True))
    weights = jnp.where(causal, jnp.exp(scores - row_max), 0.0)
    row_sum = lax.optimization_barrier(jnp.sum(weights, axis=1, keepdims=True))
    combined = jnp.dot(weights.astype(jnp.bfloat16), value_rows, preferred_element_type=jnp.float32)
    return (combined / row_sum).astype(jnp.bfloat16)

def split_heads(matrix):
    return matrix.reshape(matrix.shape[0], HEADS, HD).transpose(1, 0, 2)

def attend(queries, key_value):
    length = queries.shape[0]
    outputs = lax.map(attend_head, (split_heads(queries), split_heads(key_value[:, 0]), split_heads(key_value[:, 1])))
    return outputs.transpose(1, 0, 2).reshape(length, HEADS * HD)

def iterate(hidden_in, queries, key_value, norm_gain, w_kv, w_out):
    length = queries.shape[0]
    group_width = D // N_HEAD
    attended = attend(queries, key_value)
    attended_groups = attended.reshape(length, N_HEAD, group_width).transpose(1, 0, 2)
    weight_groups = w_out.reshape(N_HEAD, group_width, D)

    def add_group(running, pair_in):
        group_share = jnp.dot(pair_in[0], pair_in[1], preferred_element_type=jnp.float32)
        group_share = lax.optimization_barrier(group_share.astype(jnp.bfloat16)).astype(jnp.float32)
        return (running + group_share, None)
    branch_sum, unused = lax.scan(add_group, jnp.zeros((length, D), jnp.float32), (attended_groups, weight_groups))
    hidden = hidden_in.astype(jnp.float32) + branch_sum
    mean_square = lax.optimization_barrier(jnp.mean(hidden * hidden, axis=1, keepdims=True))
    normed = (hidden * lax.rsqrt(mean_square + EPSILON) * norm_gain.astype(jnp.float32)).astype(jnp.bfloat16)
    kv_product = jnp.dot(normed, w_kv.reshape(D, 2 * D), preferred_element_type=jnp.float32).reshape(length, 2, D)
    return (hidden, kv_product)

def reference(hidden_in, queries, kv_prev, norm_gain, w_kv, w_out):
    key_value = kv_prev
    for iteration in range(ITERS):
        hidden_out, kv_product = iterate(hidden_in, queries, key_value, norm_gain, w_kv, w_out)
        key_value = kv_product.astype(jnp.bfloat16)
    return (hidden_out, kv_product)
```

```python
import functools

import jax
import jax.numpy as jnp
from jax import lax
from jax.experimental import pallas as pl
from jax.experimental.pallas import tpu as pltpu
from jax.sharding import PartitionSpec as P

HD = 128
ITERS = 2
CORES = 2

MASKED = -1e30
EPSILON = 1e-05
MESH = pl.DeviceIdType.MESH


def attend_block(query, keys, values, row_start):
    scores = lax.dot_general(
        query, keys, (((1,), (1,)), ((), ())), preferred_element_type=jnp.float32
    ) * (HD ** (-0.5))
    rows = row_start + lax.broadcasted_iota(jnp.int32, scores.shape, 0)
    columns = lax.broadcasted_iota(jnp.int32, scores.shape, 1)
    scores = jnp.where(rows >= columns, scores, MASKED)
    weights = jnp.exp(scores - jnp.max(scores, axis=1, keepdims=True))
    row_sum = jnp.sum(weights, axis=1, keepdims=True)
    weighted = jnp.dot(weights.astype(jnp.bfloat16), values, preferred_element_type=jnp.float32)
    return (weighted / row_sum).astype(jnp.bfloat16)


def fused_kernel(
    n, zn, q_ref, k_ref, v_ref, hin_ref, gain_ref, wout_ref, wkv_hbm, hid_ref, kvo_ref,
    qkv, kv_next, w_pair, hin_all, a_send, a_all, p_send, rs, b_send, b_all, normed, kv_send, wkv,
    load_sem, local_sem, pair_send, pair_recv, in_send, in_recv, hin_send, hin_recv,
    a_ssem, a_rsem, p_ssem, p_rsem, b_ssem, b_rsem, g_ssem, g_rsem, kv_ssem, kv_rsem,
):
    c = lax.axis_index("ctx")
    z = lax.axis_index("head")
    core = lax.rem(c, CORES)
    k = lax.div(c, CORES)
    groups = n // CORES
    rows, width = q_ref.shape
    quarter = rows // zn
    block = rows * CORES
    chip_width = CORES * wout_ref.shape[1]
    pending = []

    def send(src, dst, ssem, rsem, where):
        copy = pltpu.make_async_remote_copy(
            src_ref=src, dst_ref=dst, send_sem=ssem, recv_sem=rsem, device_id=where, device_id_type=MESH
        )
        copy.start()
        pending.append(copy)
        return copy

    def cols(index, size):
        return pl.ds(pl.multiple_of(index * size, size), size)

    load = pltpu.make_async_copy(wkv_hbm, wkv, load_sem)
    load.start()
    own_w = pltpu.make_async_copy(wout_ref, w_pair.at[core], local_sem)
    own_w.start()

    barrier = pltpu.get_barrier_semaphore()
    for d in range(1, n):
        pl.semaphore_signal(barrier, inc=1, device_id={"ctx": lax.rem(c + d, n)}, device_id_type=MESH)
    for d in range(1, zn):
        pl.semaphore_signal(barrier, inc=1, device_id={"head": lax.rem(z + d, zn)}, device_id_type=MESH)
    pl.semaphore_wait(barrier, n - 1 + zn - 1)

    arrivals = []
    for kind, ref in ((1, k_ref), (0, q_ref), (2, v_ref)):
        for d in range(1, n):
            peer = lax.rem(c + d, n)
            arrivals.append(send(
                ref.at[:, cols(peer, HD)], qkv.at[kind, cols(c, rows)],
                in_send.at[kind, d], in_recv.at[kind, d], {"ctx": peer},
            ))
        qkv[kind, cols(c, rows), :] = ref[:, cols(c, HD)]
    pair = send(wout_ref, w_pair.at[core], pair_send, pair_recv, {"ctx": k * CORES + 1 - core})
    hin_copies = [
        send(hin_ref, hin_all.at[:, cols(z, width)], hin_send.at[d], hin_recv.at[d],
             {"head": lax.rem(z + d, zn)})
        for d in range(1, zn)
    ]
    hin_all[:, cols(z, width)] = hin_ref[...]

    for it in range(ITERS):
        for copy in arrivals:
            copy.wait_recv()
        key_ref = qkv.at[1] if it == 0 else kv_next.at[0]
        value_ref = qkv.at[2] if it == 0 else kv_next.at[1]

        a_copies = []
        for i in range(groups):
            limit = (i + 1) * block
            attended = attend_block(
                qkv[0, i * block:limit, :], key_ref[0:limit, :], value_ref[0:limit, :], i * block
            )
            for side in range(CORES):
                a_send[it, i, side] = attended[side * rows:(side + 1) * rows, :]
            for d in range(1, n):
                peer = lax.rem(c + d, n)
                a_copies.append(send(
                    a_send.at[it, i, lax.rem(peer, CORES)], a_all.at[it, i, :, cols(c, HD)],
                    a_ssem.at[it, i, d], a_rsem.at[it, i, d], {"ctx": peer},
                ))
            a_all[it, i, :, cols(c, HD)] = a_send[it, i, core]
        if it == 0:
            own_w.wait()
            pair.wait_recv()
        for copy in a_copies:
            copy.wait_recv()

        p_copies = []
        for t in range(groups):
            i = lax.rem(k + 1 + t, groups)
            half = chip_width // CORES
            for side in range(CORES):
                product = jnp.dot(
                    a_all[it, i], w_pair[side], preferred_element_type=jnp.float32
                ).astype(jnp.bfloat16)
                for s in range(zn):
                    p_send[it, i, s, :, side * half:(side + 1) * half] = product[s * quarter:(s + 1) * quarter, :]
            for d in range(1, zn):
                target = lax.rem(z + d, zn)
                p_copies.append(send(
                    p_send.at[it, i, target], rs.at[it, d - 1, i],
                    p_ssem.at[it, t, d], p_rsem.at[it, t, d], {"head": target},
                ))

        b_copies = []
        for t in range(groups):
            i = lax.rem(k + 1 + t, groups)
            total = p_send[it, i, z].astype(jnp.float32)
            for d in range(1, zn):
                p_copies[t * (zn - 1) + d - 1].wait_recv()
                total = total + rs[it, d - 1, i].astype(jnp.float32)
            total = total.astype(jnp.bfloat16)
            if t == groups - 1:
                b_all[it, z, :, cols(k, chip_width)] = total
            else:
                b_send[it, t] = total
                b_copies.append(send(
                    b_send.at[it, t], b_all.at[it, z, :, cols(k, chip_width)],
                    b_ssem.at[it, t], b_rsem.at[it, t], {"ctx": i * CORES + core},
                ))

        g_copies = []
        for t in range(groups):
            source = lax.rem(k + groups - 1 - t, groups)
            if t < groups - 1:
                b_copies[t].wait_recv()
            for d in range(1, zn):
                place = b_all.at[it, z, :, cols(source, chip_width)]
                g_copies.append(send(
                    place, place, g_ssem.at[it, t, d], g_rsem.at[it, t, d], {"head": lax.rem(z + d, zn)}
                ))
        if it == 0:
            for copy in hin_copies:
                copy.wait_recv()
        for d in range(zn):
            part = lax.rem(z + zn - d, zn)
            if d > 0:
                for t in range(groups):
                    g_copies[t * (zn - 1) + d - 1].wait_recv()
            span = cols(part, quarter)
            hidden = hin_all[span, :].astype(jnp.float32) + b_all[it, part].astype(jnp.float32)
            mean_square = jnp.mean(hidden * hidden, axis=1, keepdims=True)
            normed[span, :] = (
                hidden * lax.rsqrt(mean_square + EPSILON) * gain_ref[...].astype(jnp.float32)
            ).astype(jnp.bfloat16)
            if it == ITERS - 1:
                hid_ref[span, :] = hin_ref[span, :].astype(jnp.float32) + b_all[
                    it, part, :, cols(z, width)
                ].astype(jnp.float32)

        if it == 0:
            load.wait()
        arrivals = []
        for kind in range(2):
            @pl.loop(0, width // 256)
            def _(j):
                product = jnp.dot(
                    normed[...], wkv[kind, :, cols(j, 256)], preferred_element_type=jnp.float32
                )
                if it == ITERS - 1:
                    kvo_ref[kind, :, cols(j, 256)] = product
                else:
                    kv_send[kind, :, cols(j, 256)] = product.astype(jnp.bfloat16)

            if it < ITERS - 1:
                for d in range(1, n):
                    peer = lax.rem(c + d, n)
                    arrivals.append(send(
                        kv_send.at[kind, :, cols(peer, HD)], kv_next.at[kind, cols(c, rows)],
                        kv_ssem.at[kind, d], kv_rsem.at[kind, d], {"ctx": peer},
                    ))
                kv_next[kind, cols(c, rows), :] = kv_send[kind, :, cols(c, HD)]

    for copy in pending:
        copy.wait_send()


def fused_device(n, zn, hidden_in, queries, kv_prev, norm_gain, w_kv, w_out):
    rows, width = queries.shape
    model = w_kv.shape[0]
    tokens = rows * n
    groups = n // CORES
    quarter = rows // zn
    chip_width = CORES * w_out.shape[1]
    vmem = pl.BlockSpec(memory_space=pltpu.VMEM)
    bf16 = jnp.bfloat16
    dma = pltpu.SemaphoreType.DMA
    hidden_out, kv = pl.pallas_call(
        functools.partial(fused_kernel, n, zn),
        out_shape=(
            jax.ShapeDtypeStruct((rows, width), jnp.float32),
            jax.ShapeDtypeStruct((2, rows, width), jnp.float32),
        ),
        in_specs=[vmem] * 6 + [pl.BlockSpec(memory_space=pl.ANY)],
        out_specs=(vmem, vmem),
        scratch_shapes=[
            pltpu.VMEM((3, tokens, HD), bf16),
            pltpu.VMEM((2, tokens, HD), bf16),
            pltpu.VMEM((CORES,) + w_out.shape, bf16),
            pltpu.VMEM((rows, model), bf16),
            pltpu.VMEM((ITERS, groups, CORES, rows, HD), bf16),
            pltpu.VMEM((ITERS, groups, rows, width), bf16),
            pltpu.VMEM((ITERS, groups, zn, quarter, chip_width), bf16),
            pltpu.VMEM((ITERS, zn - 1, groups, quarter, chip_width), bf16),
            pltpu.VMEM((ITERS, groups - 1, quarter, chip_width), bf16),
            pltpu.VMEM((ITERS, zn, quarter, model), bf16),
            pltpu.VMEM((rows, model), bf16),
            pltpu.VMEM((2, rows, width), bf16),
            pltpu.VMEM((2, model, width), bf16),
            dma, dma, dma, dma,
            dma((3, n)), dma((3, n)),
            dma((zn,)), dma((zn,)),
            dma((ITERS, groups, n)), dma((ITERS, groups, n)),
            dma((ITERS, groups, zn)), dma((ITERS, groups, zn)),
            dma((ITERS, groups)), dma((ITERS, groups)),
            dma((ITERS, groups, zn)), dma((ITERS, groups, zn)),
            dma((2, n)), dma((2, n)),
        ],
        compiler_params=pltpu.CompilerParams(
            collective_id=0, has_side_effects=True, vmem_limit_bytes=56 * 1024 * 1024
        ),
    )(
        queries, kv_prev[:, 0], kv_prev[:, 1], hidden_in, norm_gain.reshape(1, model), w_out,
        w_kv.transpose(1, 0, 2),
    )
    return hidden_out, kv.transpose(1, 0, 2)


def attend_gathered(query_heads, key_value, row_start):
    row_count, head_count = query_heads.shape[:2]
    incoming = lax.all_gather(key_value, "ctx", axis=0, tiled=True)
    block_rows = incoming.shape[0]
    key_block = incoming[:, 0].reshape(block_rows, head_count, HD)
    value_block = incoming[:, 1].reshape(block_rows, head_count, HD)
    scores = (
        jnp.einsum("qhd,khd->qhk", query_heads, key_block, preferred_element_type=jnp.float32)
        * HD ** (-0.5)
    )
    positions = row_start + jnp.arange(row_count)
    allowed = (positions[:, None] >= jnp.arange(block_rows)[None, :])[:, None, :]
    scores = jnp.where(allowed, scores, MASKED)
    weights = jnp.where(allowed, jnp.exp(scores - jnp.max(scores, axis=2, keepdims=True)), 0.0)
    row_sum = jnp.sum(weights, axis=2)
    weighted = jnp.einsum(
        "qhk,khd->qhd", weights.astype(jnp.bfloat16), value_block, preferred_element_type=jnp.float32
    )
    return (weighted / row_sum[:, :, None]).astype(jnp.bfloat16).reshape(row_count, head_count * HD)


def gathered_device(hidden_in, queries, kv_prev, norm_gain, w_kv, w_out):
    row_count, local_width = queries.shape
    head_count = local_width // HD
    row_start = lax.axis_index("ctx") * row_count
    column_start = lax.axis_index("head") * local_width
    out_rows = lax.all_gather(w_out, "ctx", axis=1, tiled=True)
    kv_weights = w_kv.reshape(w_kv.shape[0], 2 * local_width)
    gain_all = norm_gain.astype(jnp.float32)
    query_heads = queries.reshape(row_count, head_count, HD)
    input_all = lax.all_gather(hidden_in, "head", axis=1, tiled=True).astype(jnp.float32)
    key_value = kv_prev
    for _ in range(ITERS):
        attended = attend_gathered(query_heads, key_value, row_start)
        partial_value = jnp.dot(attended, out_rows, preferred_element_type=jnp.float32)
        branch_sum = lax.psum(partial_value.astype(jnp.bfloat16), "head").astype(jnp.float32)
        hidden = input_all + branch_sum
        mean_square = jnp.mean(hidden * hidden, axis=1, keepdims=True)
        normed = (hidden * lax.rsqrt(mean_square + EPSILON) * gain_all).astype(jnp.bfloat16)
        fresh_kv = jnp.dot(normed, kv_weights, preferred_element_type=jnp.float32)
        hidden_out = lax.dynamic_slice_in_dim(hidden, column_start, local_width, 1)
        kv_product = fresh_kv.reshape(row_count, 2, local_width)
        key_value = kv_product.astype(jnp.bfloat16)
    return (hidden_out, kv_product)


def per_device(n, zn, *args):
    rows, width = args[1].shape
    if width == n * HD and n % CORES == 0 and rows % (16 * zn) == 0 and zn > 1:
        return fused_device(n, zn, *args)
    return gathered_device(*args)


def solution(mesh):
    in_specs = (
        P("ctx", "head"),
        P("ctx", "head"),
        P("ctx", None, "head"),
        P(),
        P(None, None, "head"),
        P("head", "ctx"),
    )
    out_specs = (P("ctx", "head"), P("ctx", None, "head"))
    return jax.shard_map(
        functools.partial(per_device, mesh.shape["ctx"], mesh.shape["head"]),
        mesh=mesh, in_specs=in_specs, out_specs=out_specs, check_vma=False,
    )
```

```python
import functools

import jax
import jax.numpy as jnp
from jax import lax
from jax.experimental import pallas as pl
from jax.experimental.pallas import tpu as pltpu
from jax.sharding import PartitionSpec as P

HD = 128
ITERS = 2
CORES = 2

MASKED = -1e30
EPSILON = 1e-05
MESH = pl.DeviceIdType.MESH


def attend_block(query, keys, values, row_start):
    scores = lax.dot_general(
        query, keys, (((1,), (1,)), ((), ())), preferred_element_type=jnp.float32
    ) * (HD ** (-0.5))
    rows = row_start + lax.broadcasted_iota(jnp.int32, scores.shape, 0)
    columns = lax.broadcasted_iota(jnp.int32, scores.shape, 1)
    scores = jnp.where(rows >= columns, scores, MASKED)
    weights = jnp.exp(scores - jnp.max(scores, axis=1, keepdims=True))
    row_sum = jnp.sum(weights, axis=1, keepdims=True)
    weighted = jnp.dot(weights.astype(jnp.bfloat16), values, preferred_element_type=jnp.float32)
    return (weighted / row_sum).astype(jnp.bfloat16)


def fused_kernel(
    n, zn, q_ref, k_ref, v_ref, hin_ref, gain_ref, wout_ref, wkv_hbm, hid_ref, kvo_ref,
    qkv, kv_next, w_pair, hin_all, a_send, a_all, p_send, rs, acc, b_send, b_all, normed, kv_send, wkv,
    load_sem, local_sem, pair_send, pair_recv, in_send, in_recv, hin_send, hin_recv,
    a_ssem, a_rsem, p_ssem, p_rsem, b_ssem, b_rsem, g_ssem, g_rsem, kv_ssem, kv_rsem,
):
    c = lax.axis_index("ctx")
    z = lax.axis_index("head")
    core = lax.rem(c, CORES)
    k = lax.div(c, CORES)
    groups = n // CORES
    rows, width = q_ref.shape
    quarter = rows // zn
    block = rows * CORES
    chip_width = CORES * wout_ref.shape[1]
    pending = []

    def remote(src, dst, ssem, rsem, where):
        return pltpu.make_async_remote_copy(
            src_ref=src, dst_ref=dst, send_sem=ssem, recv_sem=rsem, device_id=where, device_id_type=MESH
        )

    def send(*args):
        copy = remote(*args)
        copy.start()
        pending.append((None, copy))
        return copy

    def send_if(condition, copy):
        pl.when(condition)(copy.start)
        pending.append((condition, copy))

    def cols(index, size):
        return pl.ds(pl.multiple_of(index * size, size), size)

    load = pltpu.make_async_copy(wkv_hbm, wkv, load_sem)
    load.start()
    own_w = pltpu.make_async_copy(wout_ref, w_pair.at[core], local_sem)
    own_w.start()

    barrier = pltpu.get_barrier_semaphore()
    for d in range(1, n):
        pl.semaphore_signal(barrier, inc=1, device_id={"ctx": lax.rem(c + d, n)}, device_id_type=MESH)
    for d in range(1, zn):
        pl.semaphore_signal(barrier, inc=1, device_id={"head": lax.rem(z + d, zn)}, device_id_type=MESH)
    pl.semaphore_wait(barrier, n - 1 + zn - 1)

    arrivals = []
    for kind, ref in ((1, k_ref), (0, q_ref), (2, v_ref)):
        for d in range(1, n):
            peer = lax.rem(c + d, n)
            arrivals.append(send(
                ref.at[:, cols(peer, HD)], qkv.at[kind, cols(c, rows)],
                in_send.at[kind, d], in_recv.at[kind, d], {"ctx": peer},
            ))
        qkv[kind, cols(c, rows), :] = ref[:, cols(c, HD)]
    pair = send(wout_ref, w_pair.at[core], pair_send, pair_recv, {"ctx": k * CORES + 1 - core})
    hin_copies = [
        send(hin_ref, hin_all.at[:, cols(z, width)], hin_send.at[d], hin_recv.at[d],
             {"head": lax.rem(z + d, zn)})
        for d in range(1, zn)
    ]
    hin_all[:, cols(z, width)] = hin_ref[...]

    for it in range(ITERS):
        for copy in arrivals:
            copy.wait_recv()
        key_ref = qkv.at[1] if it == 0 else kv_next.at[0]
        value_ref = qkv.at[2] if it == 0 else kv_next.at[1]

        for i in range(groups):
            limit = (i + 1) * block
            attended = attend_block(
                qkv[0, i * block:limit, :], key_ref[0:limit, :], value_ref[0:limit, :], i * block
            )
            for side in range(CORES):
                a_send[it, i, side] = attended[side * rows:(side + 1) * rows, :]
        for t in range(groups):
            for d in range(1, n):
                peer = lax.rem(c + d, n)
                i = lax.rem(lax.div(peer, CORES) + 1 + t, groups)
                send(
                    a_send.at[it, i, lax.rem(peer, CORES)], a_all.at[it, i, :, cols(c, HD)],
                    a_ssem.at[it, t, d], a_rsem.at[it, t, d], {"ctx": peer},
                )
        for i in range(groups):
            a_all[it, i, :, cols(c, HD)] = a_send[it, i, core]
        if it == 0:
            own_w.wait()
            pair.wait_recv()

        def project(t):
            i = lax.rem(k + 1 + t, groups)
            half = chip_width // CORES
            for d in range(1, n):
                remote(
                    a_send.at[it, i, core], a_all.at[it, i, :, cols(c, HD)],
                    a_ssem.at[it, t, d], a_rsem.at[it, t, d], {"ctx": lax.rem(c + d, n)},
                ).wait_recv()
            for side in range(CORES):
                product = jnp.dot(
                    a_all[it, i], w_pair[side], preferred_element_type=jnp.float32
                ).astype(jnp.bfloat16)
                for s in range(zn):
                    p_send[it, t, s, :, side * half:(side + 1) * half] = product[s * quarter:(s + 1) * quarter, :]

        def step_copy(t, s, way):
            return remote(
                p_send.at[it, t, s], rs.at[it, way, t, s], p_ssem.at[it, way, t, s], p_rsem.at[it, way, t, s],
                {"head": z + 1 if way == 0 else z - 1},
            )

        def pass_sums(t):
            for j in range(zn - 1, 0, -1):
                for way in range(2):
                    s = z + j if way == 0 else z - j
                    there = s < zn if way == 0 else s >= 0
                    behind = z > 0 if way == 0 else z < zn - 1
                    copy = step_copy(t, s, way)

                    @pl.when(there & behind)
                    def _():
                        copy.wait_recv()
                        p_send[it, t, s] = (
                            p_send[it, t, s].astype(jnp.float32) + rs[it, way, t, s].astype(jnp.float32)
                        ).astype(jnp.bfloat16)

                    send_if(there, copy)

        def finish_sums(t):
            acc[...] = p_send[it, t, z].astype(jnp.float32)
            for way in range(2):
                @pl.when(z > 0 if way == 0 else z < zn - 1)
                def _():
                    step_copy(t, z, way).wait_recv()
                    acc[...] += rs[it, way, t, z].astype(jnp.float32)
            i = lax.rem(k + 1 + t, groups)
            if t == groups - 1:
                b_all[it, z, :, cols(k, chip_width)] = acc[...].astype(jnp.bfloat16)
            else:
                b_send[it, t] = acc[...].astype(jnp.bfloat16)
                b_copies.append(send(
                    b_send.at[it, t], b_all.at[it, z, :, cols(k, chip_width)],
                    b_ssem.at[it, t], b_rsem.at[it, t], {"ctx": i * CORES + core},
                ))

        def piece_copy(t, s, way):
            place = b_all.at[it, s, :, cols(lax.rem(k + groups - 1 - t, groups), chip_width)]
            return remote(
                place, place, g_ssem.at[it, way, t, s], g_rsem.at[it, way, t, s],
                {"head": z + 1 if way == 0 else z - 1},
            )

        def start_piece(t):
            if t < groups - 1:
                b_copies[t].wait_recv()
            send_if(z < zn - 1, piece_copy(t, z, 0))
            send_if(z > 0, piece_copy(t, z, 1))

        def pass_pieces(t):
            for j in range(1, zn):
                for way in range(2):
                    s = z - j if way == 0 else z + j
                    there = s >= 0 if way == 0 else s < zn
                    ahead = z < zn - 1 if way == 0 else z > 0
                    copy = piece_copy(t, s, way)

                    @pl.when(there)
                    def _():
                        copy.wait_recv()

                    send_if(there & ahead, copy)

        b_copies = []
        for stage in range(groups + 3):
            if stage < groups:
                project(stage)
                pass_sums(stage)
            if 0 <= stage - 1 < groups:
                finish_sums(stage - 1)
            if 0 <= stage - 2 < groups:
                start_piece(stage - 2)
            if 0 <= stage - 3 < groups:
                pass_pieces(stage - 3)

        if it == 0:
            for copy in hin_copies:
                copy.wait_recv()
        for part in range(zn):
            span = slice(part * quarter, (part + 1) * quarter)
            hidden = hin_all[span, :].astype(jnp.float32) + b_all[it, part].astype(jnp.float32)
            mean_square = jnp.mean(hidden * hidden, axis=1, keepdims=True)
            normed[span, :] = (
                hidden * lax.rsqrt(mean_square + EPSILON) * gain_ref[...].astype(jnp.float32)
            ).astype(jnp.bfloat16)
            if it == ITERS - 1:
                hid_ref[span, :] = hin_ref[span, :].astype(jnp.float32) + b_all[
                    it, part, :, cols(z, width)
                ].astype(jnp.float32)

        if it == 0:
            load.wait()
        arrivals = []
        for kind in range(2):
            @pl.loop(0, width // 256)
            def _(j):
                product = jnp.dot(
                    normed[...], wkv[kind, :, cols(j, 256)], preferred_element_type=jnp.float32
                )
                if it == ITERS - 1:
                    kvo_ref[kind, :, cols(j, 256)] = product
                else:
                    kv_send[kind, :, cols(j, 256)] = product.astype(jnp.bfloat16)

            if it < ITERS - 1:
                for d in range(1, n):
                    peer = lax.rem(c + d, n)
                    arrivals.append(send(
                        kv_send.at[kind, :, cols(peer, HD)], kv_next.at[kind, cols(c, rows)],
                        kv_ssem.at[kind, d], kv_rsem.at[kind, d], {"ctx": peer},
                    ))
                kv_next[kind, cols(c, rows), :] = kv_send[kind, :, cols(c, HD)]

    for condition, copy in pending:
        if condition is None:
            copy.wait_send()
        else:
            pl.when(condition)(copy.wait_send)


def fused_device(n, zn, hidden_in, queries, kv_prev, norm_gain, w_kv, w_out):
    rows, width = queries.shape
    model = w_kv.shape[0]
    tokens = rows * n
    groups = n // CORES
    quarter = rows // zn
    chip_width = CORES * w_out.shape[1]
    vmem = pl.BlockSpec(memory_space=pltpu.VMEM)
    bf16 = jnp.bfloat16
    dma = pltpu.SemaphoreType.DMA
    hidden_out, kv = pl.pallas_call(
        functools.partial(fused_kernel, n, zn),
        out_shape=(
            jax.ShapeDtypeStruct((rows, width), jnp.float32),
            jax.ShapeDtypeStruct((2, rows, width), jnp.float32),
        ),
        in_specs=[vmem] * 6 + [pl.BlockSpec(memory_space=pl.ANY)],
        out_specs=(vmem, vmem),
        scratch_shapes=[
            pltpu.VMEM((3, tokens, HD), bf16),
            pltpu.VMEM((2, tokens, HD), bf16),
            pltpu.VMEM((CORES,) + w_out.shape, bf16),
            pltpu.VMEM((rows, model), bf16),
            pltpu.VMEM((ITERS, groups, CORES, rows, HD), bf16),
            pltpu.VMEM((ITERS, groups, rows, width), bf16),
            pltpu.VMEM((ITERS, groups, zn, quarter, chip_width), bf16),
            pltpu.VMEM((ITERS, 2, groups, zn, quarter, chip_width), bf16),
            pltpu.VMEM((quarter, chip_width), jnp.float32),
            pltpu.VMEM((ITERS, groups - 1, quarter, chip_width), bf16),
            pltpu.VMEM((ITERS, zn, quarter, model), bf16),
            pltpu.VMEM((rows, model), bf16),
            pltpu.VMEM((2, rows, width), bf16),
            pltpu.VMEM((2, model, width), bf16),
            dma, dma, dma, dma,
            dma((3, n)), dma((3, n)),
            dma((zn,)), dma((zn,)),
            dma((ITERS, groups, n)), dma((ITERS, groups, n)),
            dma((ITERS, 2, groups, zn)), dma((ITERS, 2, groups, zn)),
            dma((ITERS, groups)), dma((ITERS, groups)),
            dma((ITERS, 2, groups, zn)), dma((ITERS, 2, groups, zn)),
            dma((2, n)), dma((2, n)),
        ],
        compiler_params=pltpu.CompilerParams(
            collective_id=0, has_side_effects=True, vmem_limit_bytes=56 * 1024 * 1024
        ),
    )(
        queries, kv_prev[:, 0], kv_prev[:, 1], hidden_in, norm_gain.reshape(1, model), w_out,
        w_kv.transpose(1, 0, 2),
    )
    return hidden_out, kv.transpose(1, 0, 2)


def attend_gathered(query_heads, key_value, row_start):
    row_count, head_count = query_heads.shape[:2]
    incoming = lax.all_gather(key_value, "ctx", axis=0, tiled=True)
    block_rows = incoming.shape[0]
    key_block = incoming[:, 0].reshape(block_rows, head_count, HD)
    value_block = incoming[:, 1].reshape(block_rows, head_count, HD)
    scores = (
        jnp.einsum("qhd,khd->qhk", query_heads, key_block, preferred_element_type=jnp.float32)
        * HD ** (-0.5)
    )
    positions = row_start + jnp.arange(row_count)
    allowed = (positions[:, None] >= jnp.arange(block_rows)[None, :])[:, None, :]
    scores = jnp.where(allowed, scores, MASKED)
    weights = jnp.where(allowed, jnp.exp(scores - jnp.max(scores, axis=2, keepdims=True)), 0.0)
    row_sum = jnp.sum(weights, axis=2)
    weighted = jnp.einsum(
        "qhk,khd->qhd", weights.astype(jnp.bfloat16), value_block, preferred_element_type=jnp.float32
    )
    return (weighted / row_sum[:, :, None]).astype(jnp.bfloat16).reshape(row_count, head_count * HD)


def gathered_device(hidden_in, queries, kv_prev, norm_gain, w_kv, w_out):
    row_count, local_width = queries.shape
    head_count = local_width // HD
    row_start = lax.axis_index("ctx") * row_count
    column_start = lax.axis_index("head") * local_width
    out_rows = lax.all_gather(w_out, "ctx", axis=1, tiled=True)
    kv_weights = w_kv.reshape(w_kv.shape[0], 2 * local_width)
    gain_all = norm_gain.astype(jnp.float32)
    query_heads = queries.reshape(row_count, head_count, HD)
    input_all = lax.all_gather(hidden_in, "head", axis=1, tiled=True).astype(jnp.float32)
    key_value = kv_prev
    for _ in range(ITERS):
        attended = attend_gathered(query_heads, key_value, row_start)
        partial_value = jnp.dot(attended, out_rows, preferred_element_type=jnp.float32)
        branch_sum = lax.psum(partial_value.astype(jnp.bfloat16), "head").astype(jnp.float32)
        hidden = input_all + branch_sum
        mean_square = jnp.mean(hidden * hidden, axis=1, keepdims=True)
        normed = (hidden * lax.rsqrt(mean_square + EPSILON) * gain_all).astype(jnp.bfloat16)
        fresh_kv = jnp.dot(normed, kv_weights, preferred_element_type=jnp.float32)
        hidden_out = lax.dynamic_slice_in_dim(hidden, column_start, local_width, 1)
        kv_product = fresh_kv.reshape(row_count, 2, local_width)
        key_value = kv_product.astype(jnp.bfloat16)
    return (hidden_out, kv_product)


def per_device(n, zn, *args):
    rows, width = args[1].shape
    if width == n * HD and n % CORES == 0 and rows % (16 * zn) == 0 and zn > 1:
        return fused_device(n, zn, *args)
    return gathered_device(*args)


def solution(mesh):
    in_specs = (
        P("ctx", "head"),
        P("ctx", "head"),
        P("ctx", None, "head"),
        P(),
        P(None, None, "head"),
        P("head", "ctx"),
    )
    out_specs = (P("ctx", "head"), P("ctx", None, "head"))
    return jax.shard_map(
        functools.partial(per_device, mesh.shape["ctx"], mesh.shape["head"]),
        mesh=mesh, in_specs=in_specs, out_specs=out_specs, check_vma=False,
    )
```

```python
import functools

import jax
import jax.numpy as jnp
from jax import lax
from jax.experimental import pallas as pl
from jax.experimental.pallas import tpu as pltpu
from jax.sharding import PartitionSpec as P

HD = 128
ITERS = 2
CORES = 2

MASKED = -1e30
EPSILON = 1e-05
MESH = pl.DeviceIdType.MESH


def attend_block(query, keys, values, row_start):
    scores = lax.dot_general(
        query, keys, (((1,), (1,)), ((), ())), preferred_element_type=jnp.float32
    ) * (HD ** (-0.5))
    rows = row_start + lax.broadcasted_iota(jnp.int32, scores.shape, 0)
    columns = lax.broadcasted_iota(jnp.int32, scores.shape, 1)
    scores = jnp.where(rows >= columns, scores, MASKED)
    weights = jnp.exp(scores - jnp.max(scores, axis=1, keepdims=True))
    row_sum = jnp.sum(weights, axis=1, keepdims=True)
    weighted = jnp.dot(weights.astype(jnp.bfloat16), values, preferred_element_type=jnp.float32)
    return (weighted / row_sum).astype(jnp.bfloat16)


def fused_kernel(
    n, zn, q_ref, kv_ref, hin_ref, gain_ref, wout_ref, wkv_hbm, hid_ref, kvo_ref,
    q_all, kv_land, kv_all, w_pair, hin_all, a_send, a_all, p_send, rs, acc, b_send, b_all, scaled, squares, kv_acc, kv_send, wkv,
    load_sem, local_sem, pair_send, pair_recv, in_send, in_recv, hin_send, hin_recv,
    a_ssem, a_rsem, p_ssem, p_rsem, b_ssem, b_rsem, g_ssem, g_rsem, kv_ssem, kv_rsem,
):
    c = lax.axis_index("ctx")
    z = lax.axis_index("head")
    core = lax.rem(c, CORES)
    k = lax.div(c, CORES)
    groups = n // CORES
    rows, width = q_ref.shape
    quarter = rows // zn
    block = rows * CORES
    chip_width = CORES * wout_ref.shape[1]
    pending = []

    def remote(src, dst, ssem, rsem, where):
        return pltpu.make_async_remote_copy(
            src_ref=src, dst_ref=dst, send_sem=ssem, recv_sem=rsem, device_id=where, device_id_type=MESH
        )

    def send(*args):
        copy = remote(*args)
        copy.start()
        pending.append((None, copy))
        return copy

    def send_if(condition, copy):
        pl.when(condition)(copy.start)
        pending.append((condition, copy))

    def cols(index, size):
        return pl.ds(pl.multiple_of(index * size, size), size)

    load = pltpu.make_async_copy(wkv_hbm, wkv, load_sem)
    load.start()
    own_w = pltpu.make_async_copy(wout_ref, w_pair.at[core], local_sem)
    own_w.start()

    barrier = pltpu.get_barrier_semaphore()
    for d in range(1, n):
        pl.semaphore_signal(barrier, inc=1, device_id={"ctx": lax.rem(c + d, n)}, device_id_type=MESH)
    for d in range(1, zn):
        pl.semaphore_signal(barrier, inc=1, device_id={"head": lax.rem(z + d, zn)}, device_id_type=MESH)
    pl.semaphore_wait(barrier, n - 1 + zn - 1)

    arrivals = []
    for d in range(1, n):
        peer = lax.rem(c + d, n)
        arrivals.append(send(
            kv_ref.at[:, :, cols(peer, HD)], kv_land.at[cols(c, rows)],
            in_send.at[0, d], in_recv.at[0, d], {"ctx": peer},
        ))
        arrivals.append(send(
            q_ref.at[:, cols(peer, HD)], q_all.at[cols(c, rows)],
            in_send.at[1, d], in_recv.at[1, d], {"ctx": peer},
        ))
    kv_land[cols(c, rows), :, :] = kv_ref[:, :, cols(c, HD)]
    q_all[cols(c, rows), :] = q_ref[:, cols(c, HD)]
    pair = send(wout_ref, w_pair.at[core], pair_send, pair_recv, {"ctx": k * CORES + 1 - core})
    hin_copies = [
        send(hin_ref, hin_all.at[:, cols(z, width)], hin_send.at[d], hin_recv.at[d],
             {"head": lax.rem(z + d, zn)})
        for d in range(1, zn)
    ]
    hin_all[:, cols(z, width)] = hin_ref[...]

    for it in range(ITERS):
        for copy in arrivals:
            copy.wait_recv()
        if it == 0:
            for kind in range(2):
                kv_all[it, kind] = kv_land[:, kind, :]

        for i in range(groups):
            limit = (i + 1) * block
            attended = attend_block(
                q_all[i * block:limit, :], kv_all[it, 0, 0:limit, :], kv_all[it, 1, 0:limit, :], i * block
            )
            for side in range(CORES):
                a_send[it, i, side] = attended[side * rows:(side + 1) * rows, :]
        for t in range(groups):
            for d in range(1, n):
                peer = lax.rem(c + d, n)
                i = lax.rem(lax.div(peer, CORES) + 1 + t, groups)
                send(
                    a_send.at[it, i, lax.rem(peer, CORES)], a_all.at[it, i, :, cols(c, HD)],
                    a_ssem.at[it, t, d], a_rsem.at[it, t, d], {"ctx": peer},
                )
        for i in range(groups):
            a_all[it, i, :, cols(c, HD)] = a_send[it, i, core]
        if it == 0:
            own_w.wait()
            pair.wait_recv()

        def project(t):
            i = lax.rem(k + 1 + t, groups)
            half = chip_width // CORES
            for d in range(1, n):
                remote(
                    a_send.at[it, i, core], a_all.at[it, i, :, cols(c, HD)],
                    a_ssem.at[it, t, d], a_rsem.at[it, t, d], {"ctx": lax.rem(c + d, n)},
                ).wait_recv()
            for side in range(CORES):
                product = jnp.dot(
                    a_all[it, i], w_pair[side], preferred_element_type=jnp.float32
                ).astype(jnp.bfloat16)
                for s in range(zn):
                    p_send[it, t, s, :, side * half:(side + 1) * half] = product[s * quarter:(s + 1) * quarter, :]

        def step_copy(t, s, way):
            return remote(
                p_send.at[it, t, s], rs.at[it, way, t, s], p_ssem.at[it, way, t, s], p_rsem.at[it, way, t, s],
                {"head": z + 1 if way == 0 else z - 1},
            )

        def pass_sums(t):
            for j in range(zn - 1, 0, -1):
                for way in range(2):
                    s = z + j if way == 0 else z - j
                    there = s < zn if way == 0 else s >= 0
                    behind = z > 0 if way == 0 else z < zn - 1
                    copy = step_copy(t, s, way)

                    @pl.when(there & behind)
                    def _():
                        copy.wait_recv()
                        p_send[it, t, s] = (
                            p_send[it, t, s].astype(jnp.float32) + rs[it, way, t, s].astype(jnp.float32)
                        ).astype(jnp.bfloat16)

                    send_if(there, copy)

        def finish_sums(t):
            acc[...] = p_send[it, t, z].astype(jnp.float32)
            for way in range(2):
                @pl.when(z > 0 if way == 0 else z < zn - 1)
                def _():
                    step_copy(t, z, way).wait_recv()
                    acc[...] += rs[it, way, t, z].astype(jnp.float32)
            i = lax.rem(k + 1 + t, groups)
            if t == groups - 1:
                b_all[it, z, :, cols(k, chip_width)] = acc[...].astype(jnp.bfloat16)
            else:
                b_send[it, t] = acc[...].astype(jnp.bfloat16)
                b_copies.append(send(
                    b_send.at[it, t], b_all.at[it, z, :, cols(k, chip_width)],
                    b_ssem.at[it, t], b_rsem.at[it, t], {"ctx": i * CORES + core},
                ))

        def piece_copy(t, s, way):
            place = b_all.at[it, s, :, cols(lax.rem(k + groups - 1 - t, groups), chip_width)]
            return remote(
                place, place, g_ssem.at[it, way, t, s], g_rsem.at[it, way, t, s],
                {"head": z + 1 if way == 0 else z - 1},
            )

        def start_piece(t):
            if t < groups - 1:
                b_copies[t].wait_recv()
            send_if(z < zn - 1, piece_copy(t, z, 0))
            send_if(z > 0, piece_copy(t, z, 1))

        def pass_pieces(t):
            for j in range(1, zn):
                for way in range(2):
                    s = z - j if way == 0 else z + j
                    there = s >= 0 if way == 0 else s < zn
                    ahead = z < zn - 1 if way == 0 else z > 0
                    copy = piece_copy(t, s, way)

                    @pl.when(there)
                    def _():
                        copy.wait_recv()

                    send_if(there & ahead, copy)

        def consume(t):
            place = cols(lax.rem(k + groups - 1 - t, groups), chip_width)
            hidden = hin_all[:, place].astype(jnp.float32) + b_all[it, :, :, place].astype(
                jnp.float32
            ).reshape(rows, chip_width)
            square = jnp.sum(hidden * hidden, axis=1, keepdims=True)
            scaled[...] = (hidden * gain_ref[:, place].astype(jnp.float32)).astype(jnp.bfloat16)
            squares[...] = square if t == 0 else squares[...] + square
            scale = lax.rsqrt(squares[...] / hin_all.shape[1] + EPSILON)
            copies = []
            for kind in range(2):
                @pl.loop(0, width // 256)
                def _(j):
                    product = jnp.dot(
                        scaled[...], wkv[kind, place, cols(j, 256)], preferred_element_type=jnp.float32
                    )
                    if t > 0:
                        product = product + kv_acc[kind, :, cols(j, 256)]
                    if t < groups - 1:
                        kv_acc[kind, :, cols(j, 256)] = product
                    elif it == ITERS - 1:
                        kvo_ref[:, kind, cols(j, 256)] = product * scale
                    else:
                        kv_send[kind, :, cols(j, 256)] = (product * scale).astype(jnp.bfloat16)

                if t == groups - 1 and it < ITERS - 1:
                    for d in range(1, n):
                        peer = lax.rem(c + d, n)
                        copies.append(send(
                            kv_send.at[kind, :, cols(peer, HD)], kv_all.at[it + 1, kind, cols(c, rows)],
                            kv_ssem.at[kind, d], kv_rsem.at[kind, d], {"ctx": peer},
                        ))
                    kv_all[it + 1, kind, cols(c, rows), :] = kv_send[kind, :, cols(c, HD)]
            return copies

        b_copies = []
        for stage in range(groups + 3):
            if stage < groups:
                project(stage)
                pass_sums(stage)
            if 0 <= stage - 1 < groups:
                finish_sums(stage - 1)
            if 0 <= stage - 2 < groups:
                start_piece(stage - 2)
            if it == 0 and stage == 4:
                for copy in hin_copies:
                    copy.wait_recv()
                load.wait()
            if stage - 4 == groups - 2:
                consume(stage - 4)
            if 0 <= stage - 3 < groups:
                pass_pieces(stage - 3)
            if 0 <= stage - 4 < groups - 2:
                consume(stage - 4)
        arrivals = consume(groups - 1)
        if it == ITERS - 1:
            hid_ref[...] = hin_ref[...].astype(jnp.float32) + b_all[it, :, :, cols(z, width)].astype(
                jnp.float32
            ).reshape(rows, width)

    for condition, copy in pending:
        if condition is None:
            copy.wait_send()
        else:
            pl.when(condition)(copy.wait_send)


def fused_device(n, zn, hidden_in, queries, kv_prev, norm_gain, w_kv, w_out):
    rows, width = queries.shape
    model = w_kv.shape[0]
    tokens = rows * n
    groups = n // CORES
    quarter = rows // zn
    chip_width = CORES * w_out.shape[1]
    vmem = pl.BlockSpec(memory_space=pltpu.VMEM)
    bf16 = jnp.bfloat16
    dma = pltpu.SemaphoreType.DMA
    return pl.pallas_call(
        functools.partial(fused_kernel, n, zn),
        out_shape=(
            jax.ShapeDtypeStruct((rows, width), jnp.float32),
            jax.ShapeDtypeStruct((rows, 2, width), jnp.float32),
        ),
        in_specs=[vmem] * 5 + [pl.BlockSpec(memory_space=pl.ANY)],
        out_specs=(vmem, vmem),
        scratch_shapes=[
            pltpu.VMEM((tokens, HD), bf16),
            pltpu.VMEM((tokens, 2, HD), bf16),
            pltpu.VMEM((ITERS, 2, tokens, HD), bf16),
            pltpu.VMEM((CORES,) + w_out.shape, bf16),
            pltpu.VMEM((rows, model), bf16),
            pltpu.VMEM((ITERS, groups, CORES, rows, HD), bf16),
            pltpu.VMEM((ITERS, groups, rows, width), bf16),
            pltpu.VMEM((ITERS, groups, zn, quarter, chip_width), bf16),
            pltpu.VMEM((ITERS, 2, groups, zn, quarter, chip_width), bf16),
            pltpu.VMEM((quarter, chip_width), jnp.float32),
            pltpu.VMEM((ITERS, groups - 1, quarter, chip_width), bf16),
            pltpu.VMEM((ITERS, zn, quarter, model), bf16),
            pltpu.VMEM((rows, chip_width), bf16),
            pltpu.VMEM((rows, 1), jnp.float32),
            pltpu.VMEM((2, rows, width), jnp.float32),
            pltpu.VMEM((2, rows, width), bf16),
            pltpu.VMEM((2, model, width), bf16),
            dma, dma, dma, dma,
            dma((2, n)), dma((2, n)),
            dma((zn,)), dma((zn,)),
            dma((ITERS, groups, n)), dma((ITERS, groups, n)),
            dma((ITERS, 2, groups, zn)), dma((ITERS, 2, groups, zn)),
            dma((ITERS, groups)), dma((ITERS, groups)),
            dma((ITERS, 2, groups, zn)), dma((ITERS, 2, groups, zn)),
            dma((2, n)), dma((2, n)),
        ],
        compiler_params=pltpu.CompilerParams(
            collective_id=0, has_side_effects=True, vmem_limit_bytes=58 * 1024 * 1024
        ),
    )(queries, kv_prev, hidden_in, norm_gain.reshape(1, model), w_out, w_kv.transpose(1, 0, 2))


def attend_gathered(query_heads, key_value, row_start):
    row_count, head_count = query_heads.shape[:2]
    incoming = lax.all_gather(key_value, "ctx", axis=0, tiled=True)
    block_rows = incoming.shape[0]
    key_block = incoming[:, 0].reshape(block_rows, head_count, HD)
    value_block = incoming[:, 1].reshape(block_rows, head_count, HD)
    scores = (
        jnp.einsum("qhd,khd->qhk", query_heads, key_block, preferred_element_type=jnp.float32)
        * HD ** (-0.5)
    )
    positions = row_start + jnp.arange(row_count)
    allowed = (positions[:, None] >= jnp.arange(block_rows)[None, :])[:, None, :]
    scores = jnp.where(allowed, scores, MASKED)
    weights = jnp.where(allowed, jnp.exp(scores - jnp.max(scores, axis=2, keepdims=True)), 0.0)
    row_sum = jnp.sum(weights, axis=2)
    weighted = jnp.einsum(
        "qhk,khd->qhd", weights.astype(jnp.bfloat16), value_block, preferred_element_type=jnp.float32
    )
    return (weighted / row_sum[:, :, None]).astype(jnp.bfloat16).reshape(row_count, head_count * HD)


def gathered_device(hidden_in, queries, kv_prev, norm_gain, w_kv, w_out):
    row_count, local_width = queries.shape
    head_count = local_width // HD
    row_start = lax.axis_index("ctx") * row_count
    column_start = lax.axis_index("head") * local_width
    out_rows = lax.all_gather(w_out, "ctx", axis=1, tiled=True)
    kv_weights = w_kv.reshape(w_kv.shape[0], 2 * local_width)
    gain_all = norm_gain.astype(jnp.float32)
    query_heads = queries.reshape(row_count, head_count, HD)
    input_all = lax.all_gather(hidden_in, "head", axis=1, tiled=True).astype(jnp.float32)
    key_value = kv_prev
    for _ in range(ITERS):
        attended = attend_gathered(query_heads, key_value, row_start)
        partial_value = jnp.dot(attended, out_rows, preferred_element_type=jnp.float32)
        branch_sum = lax.psum(partial_value.astype(jnp.bfloat16), "head").astype(jnp.float32)
        hidden = input_all + branch_sum
        mean_square = jnp.mean(hidden * hidden, axis=1, keepdims=True)
        normed = (hidden * lax.rsqrt(mean_square + EPSILON) * gain_all).astype(jnp.bfloat16)
        fresh_kv = jnp.dot(normed, kv_weights, preferred_element_type=jnp.float32)
        hidden_out = lax.dynamic_slice_in_dim(hidden, column_start, local_width, 1)
        kv_product = fresh_kv.reshape(row_count, 2, local_width)
        key_value = kv_product.astype(jnp.bfloat16)
    return (hidden_out, kv_product)


def per_device(n, zn, *args):
    rows, width = args[1].shape
    if width == n * HD and n % CORES == 0 and rows % (16 * zn) == 0 and zn > 1:
        return fused_device(n, zn, *args)
    return gathered_device(*args)


def solution(mesh):
    in_specs = (
        P("ctx", "head"),
        P("ctx", "head"),
        P("ctx", None, "head"),
        P(),
        P(None, None, "head"),
        P("head", "ctx"),
    )
    out_specs = (P("ctx", "head"), P("ctx", None, "head"))
    return jax.shard_map(
        functools.partial(per_device, mesh.shape["ctx"], mesh.shape["head"]),
        mesh=mesh, in_specs=in_specs, out_specs=out_specs, check_vma=False,
    )
```

```python
import functools

import jax
import jax.numpy as jnp
from jax import lax
from jax.experimental import pallas as pl
from jax.experimental.pallas import tpu as pltpu
from jax.sharding import PartitionSpec as P

HD = 128
ITERS = 2
CORES = 2

MASKED = -1e30
EPSILON = 1e-05
MESH = pl.DeviceIdType.MESH


def attend_block(query, keys, values, row_start):
    scores = lax.dot_general(
        query, keys, (((1,), (1,)), ((), ())), preferred_element_type=jnp.float32
    ) * (HD ** (-0.5))
    rows = row_start + lax.broadcasted_iota(jnp.int32, scores.shape, 0)
    columns = lax.broadcasted_iota(jnp.int32, scores.shape, 1)
    scores = jnp.where(rows >= columns, scores, MASKED)
    weights = jnp.exp(scores - jnp.max(scores, axis=1, keepdims=True))
    row_sum = jnp.sum(weights, axis=1, keepdims=True)
    weighted = jnp.dot(weights.astype(jnp.bfloat16), values, preferred_element_type=jnp.float32)
    return (weighted / row_sum).astype(jnp.bfloat16)


def fused_kernel(
    n, zn, q_ref, kv_ref, hin_ref, gain_ref, wout_ref, wkv_hbm, hid_ref, kvo_ref,
    q_all, kv_land, kv_all, w_pair, hin_all, a_send, a_all, p_send, rs, acc, b_send, b_all, scaled, squares, kv_acc, kv_send, wkv,
    load_sem, local_sem, pair_send, pair_recv, in_send, in_recv, hin_send, hin_recv,
    a_ssem, a_rsem, p_ssem, p_rsem, b_ssem, b_rsem, g_ssem, g_rsem, kv_ssem, kv_rsem,
):
    c = lax.axis_index("ctx")
    z = lax.axis_index("head")
    core = lax.rem(c, CORES)
    k = lax.div(c, CORES)
    groups = n // CORES
    rows, width = q_ref.shape
    quarter = rows // zn
    block = rows * CORES
    chip_width = CORES * wout_ref.shape[1]
    pending = []

    def remote(src, dst, ssem, rsem, where):
        return pltpu.make_async_remote_copy(
            src_ref=src, dst_ref=dst, send_sem=ssem, recv_sem=rsem, device_id=where, device_id_type=MESH
        )

    def send(*args):
        copy = remote(*args)
        copy.start()
        pending.append((None, copy))
        return copy

    def send_if(condition, copy):
        pl.when(condition)(copy.start)
        pending.append((condition, copy))

    def cols(index, size):
        return pl.ds(pl.multiple_of(index * size, size), size)

    load = pltpu.make_async_copy(wkv_hbm, wkv, load_sem)
    load.start()
    own_w = pltpu.make_async_copy(wout_ref, w_pair.at[core], local_sem)
    own_w.start()

    barrier = pltpu.get_barrier_semaphore()
    for d in range(1, n):
        pl.semaphore_signal(barrier, inc=1, device_id={"ctx": lax.rem(c + d, n)}, device_id_type=MESH)
    for d in range(1, zn):
        pl.semaphore_signal(barrier, inc=1, device_id={"head": lax.rem(z + d, zn)}, device_id_type=MESH)
    pl.semaphore_wait(barrier, n - 1 + zn - 1)

    arrivals = []
    for d in range(1, n):
        peer = lax.rem(c + d, n)
        arrivals.append(send(
            kv_ref.at[:, :, cols(peer, HD)], kv_land.at[cols(c, rows)],
            in_send.at[0, d], in_recv.at[0, d], {"ctx": peer},
        ))
        arrivals.append(send(
            q_ref.at[:, cols(peer, HD)], q_all.at[cols(c, rows)],
            in_send.at[1, d], in_recv.at[1, d], {"ctx": peer},
        ))
    kv_land[cols(c, rows), :, :] = kv_ref[:, :, cols(c, HD)]
    q_all[cols(c, rows), :] = q_ref[:, cols(c, HD)]
    pair = send(wout_ref, w_pair.at[core], pair_send, pair_recv, {"ctx": k * CORES + 1 - core})
    hin_copies = [
        send(hin_ref, hin_all.at[:, cols(z, width)], hin_send.at[d], hin_recv.at[d],
             {"head": lax.rem(z + d, zn)})
        for d in range(1, zn)
    ]
    hin_all[:, cols(z, width)] = hin_ref[...]

    for it in range(ITERS):
        for copy in arrivals:
            copy.wait_recv()
        if it == 0:
            for kind in range(2):
                kv_all[it, kind] = kv_land[:, kind, :]

        for i in range(groups):
            limit = (i + 1) * block
            attended = attend_block(
                q_all[i * block:limit, :], kv_all[it, 0, 0:limit, :], kv_all[it, 1, 0:limit, :], i * block
            )
            for side in range(CORES):
                a_send[it, i, side] = attended[side * rows:(side + 1) * rows, :]
        for t in range(groups):
            for d in range(1, n):
                peer = lax.rem(c + d, n)
                i = lax.rem(lax.div(peer, CORES) + 1 + t, groups)
                send(
                    a_send.at[it, i, lax.rem(peer, CORES)], a_all.at[it, i, :, cols(c, HD)],
                    a_ssem.at[it, t, d], a_rsem.at[it, t, d], {"ctx": peer},
                )
        for i in range(groups):
            a_all[it, i, :, cols(c, HD)] = a_send[it, i, core]
        if it == 0:
            own_w.wait()
            pair.wait_recv()

        def project(t):
            i = lax.rem(k + 1 + t, groups)
            half = chip_width // CORES
            for d in range(1, n):
                remote(
                    a_send.at[it, i, core], a_all.at[it, i, :, cols(c, HD)],
                    a_ssem.at[it, t, d], a_rsem.at[it, t, d], {"ctx": lax.rem(c + d, n)},
                ).wait_recv()
            for side in range(CORES):
                product = jnp.dot(
                    a_all[it, i], w_pair[side], preferred_element_type=jnp.float32
                ).astype(jnp.bfloat16)
                for s in range(zn):
                    p_send[it, t, s, :, side * half:(side + 1) * half] = product[s * quarter:(s + 1) * quarter, :]

        def step_copy(t, s, way):
            return remote(
                p_send.at[it, t, s], rs.at[it, way, t, s], p_ssem.at[it, way, t, s], p_rsem.at[it, way, t, s],
                {"head": z + 1 if way == 0 else z - 1},
            )

        def pass_sums(t, hop):
            for way in range(2):
                @pl.when(z == (hop if way == 0 else zn - 1 - hop))
                def _():
                    for j in range(zn - 1 - hop, 0, -1):
                        s = hop + j if way == 0 else zn - 1 - hop - j
                        copy = step_copy(t, s, way)
                        if hop > 0:
                            copy.wait_recv()
                            p_send[it, t, s] = (
                                p_send[it, t, s].astype(jnp.float32) + rs[it, way, t, s].astype(jnp.float32)
                            ).astype(jnp.bfloat16)
                        copy.start()

                for j in range(zn - 1 - hop, 0, -1):
                    s = hop + j if way == 0 else zn - 1 - hop - j
                    pending.append((z == (hop if way == 0 else zn - 1 - hop), step_copy(t, s, way)))

        def finish_sums(t):
            acc[...] = p_send[it, t, z].astype(jnp.float32)
            for way in range(2):
                @pl.when(z > 0 if way == 0 else z < zn - 1)
                def _():
                    step_copy(t, z, way).wait_recv()
                    acc[...] += rs[it, way, t, z].astype(jnp.float32)
            i = lax.rem(k + 1 + t, groups)
            if t == groups - 1:
                b_all[it, z, :, cols(k, chip_width)] = acc[...].astype(jnp.bfloat16)
            else:
                b_send[it, t] = acc[...].astype(jnp.bfloat16)
                b_copies.append(send(
                    b_send.at[it, t], b_all.at[it, z, :, cols(k, chip_width)],
                    b_ssem.at[it, t], b_rsem.at[it, t], {"ctx": i * CORES + core},
                ))

        def piece_copy(t, s, way):
            place = b_all.at[it, s, :, cols(lax.rem(k + groups - 1 - t, groups), chip_width)]
            return remote(
                place, place, g_ssem.at[it, way, t, s], g_rsem.at[it, way, t, s],
                {"head": z + 1 if way == 0 else z - 1},
            )

        def start_piece(t):
            if t < groups - 1:
                b_copies[t].wait_recv()
            send_if(z < zn - 1, piece_copy(t, z, 0))
            send_if(z > 0, piece_copy(t, z, 1))

        def pass_pieces(t, j):
            for way in range(2):
                s = z - j if way == 0 else z + j
                there = s >= 0 if way == 0 else s < zn
                ahead = z < zn - 1 if way == 0 else z > 0
                copy = piece_copy(t, s, way)
                pl.when(there)(copy.wait_recv)
                send_if(there & ahead, copy)

        def consume(t):
            place = cols(lax.rem(k + groups - 1 - t, groups), chip_width)
            hidden = hin_all[:, place].astype(jnp.float32) + b_all[it, :, :, place].astype(
                jnp.float32
            ).reshape(rows, chip_width)
            square = jnp.sum(hidden * hidden, axis=1, keepdims=True)
            scaled[...] = (hidden * gain_ref[:, place].astype(jnp.float32)).astype(jnp.bfloat16)
            squares[...] = square if t == 0 else squares[...] + square
            scale = lax.rsqrt(squares[...] / hin_all.shape[1] + EPSILON)
            copies = []
            for kind in range(2):
                @pl.loop(0, width // 256)
                def _(j):
                    product = jnp.dot(
                        scaled[...], wkv[kind, place, cols(j, 256)], preferred_element_type=jnp.float32
                    )
                    if t > 0:
                        product = product + kv_acc[kind, :, cols(j, 256)]
                    if t < groups - 1:
                        kv_acc[kind, :, cols(j, 256)] = product
                    elif it == ITERS - 1:
                        kvo_ref[:, kind, cols(j, 256)] = product * scale
                    else:
                        kv_send[kind, :, cols(j, 256)] = (product * scale).astype(jnp.bfloat16)

                if t == groups - 1 and it < ITERS - 1:
                    for d in range(1, n):
                        peer = lax.rem(c + d, n)
                        copies.append(send(
                            kv_send.at[kind, :, cols(peer, HD)], kv_all.at[it + 1, kind, cols(c, rows)],
                            kv_ssem.at[kind, d], kv_rsem.at[kind, d], {"ctx": peer},
                        ))
                    kv_all[it + 1, kind, cols(c, rows), :] = kv_send[kind, :, cols(c, HD)]
            return copies

        b_copies = []
        tasks = [project]
        tasks += [functools.partial(pass_sums, hop=hop) for hop in range(zn - 1)]
        tasks += [finish_sums, start_piece]
        tasks += [functools.partial(pass_pieces, j=j) for j in range(1, zn)]
        lags = [0] + list(range(zn - 1)) + list(range(zn - 1, 2 * zn))
        for stage in range(groups + 2 * zn):
            for task, lag in zip(tasks, lags):
                if 0 <= stage - lag < groups:
                    task(stage - lag)
            if stage == 2 * zn and it == 0:
                for copy in hin_copies:
                    copy.wait_recv()
                load.wait()
            if 0 <= stage - 2 * zn < groups - 1:
                consume(stage - 2 * zn)
        arrivals = consume(groups - 1)
        if it == ITERS - 1:
            hid_ref[...] = hin_ref[...].astype(jnp.float32) + b_all[it, :, :, cols(z, width)].astype(
                jnp.float32
            ).reshape(rows, width)

    for condition, copy in pending:
        if condition is None:
            copy.wait_send()
        else:
            pl.when(condition)(copy.wait_send)


def fused_device(n, zn, hidden_in, queries, kv_prev, norm_gain, w_kv, w_out):
    rows, width = queries.shape
    model = w_kv.shape[0]
    tokens = rows * n
    groups = n // CORES
    quarter = rows // zn
    chip_width = CORES * w_out.shape[1]
    vmem = pl.BlockSpec(memory_space=pltpu.VMEM)
    bf16 = jnp.bfloat16
    dma = pltpu.SemaphoreType.DMA
    return pl.pallas_call(
        functools.partial(fused_kernel, n, zn),
        out_shape=(
            jax.ShapeDtypeStruct((rows, width), jnp.float32),
            jax.ShapeDtypeStruct((rows, 2, width), jnp.float32),
        ),
        in_specs=[vmem] * 5 + [pl.BlockSpec(memory_space=pl.ANY)],
        out_specs=(vmem, vmem),
        scratch_shapes=[
            pltpu.VMEM((tokens, HD), bf16),
            pltpu.VMEM((tokens, 2, HD), bf16),
            pltpu.VMEM((ITERS, 2, tokens, HD), bf16),
            pltpu.VMEM((CORES,) + w_out.shape, bf16),
            pltpu.VMEM((rows, model), bf16),
            pltpu.VMEM((ITERS, groups, CORES, rows, HD), bf16),
            pltpu.VMEM((ITERS, groups, rows, width), bf16),
            pltpu.VMEM((ITERS, groups, zn, quarter, chip_width), bf16),
            pltpu.VMEM((ITERS, 2, groups, zn, quarter, chip_width), bf16),
            pltpu.VMEM((quarter, chip_width), jnp.float32),
            pltpu.VMEM((ITERS, groups - 1, quarter, chip_width), bf16),
            pltpu.VMEM((ITERS, zn, quarter, model), bf16),
            pltpu.VMEM((rows, chip_width), bf16),
            pltpu.VMEM((rows, 1), jnp.float32),
            pltpu.VMEM((2, rows, width), jnp.float32),
            pltpu.VMEM((2, rows, width), bf16),
            pltpu.VMEM((2, model, width), bf16),
            dma, dma, dma, dma,
            dma((2, n)), dma((2, n)),
            dma((zn,)), dma((zn,)),
            dma((ITERS, groups, n)), dma((ITERS, groups, n)),
            dma((ITERS, 2, groups, zn)), dma((ITERS, 2, groups, zn)),
            dma((ITERS, groups)), dma((ITERS, groups)),
            dma((ITERS, 2, groups, zn)), dma((ITERS, 2, groups, zn)),
            dma((2, n)), dma((2, n)),
        ],
        compiler_params=pltpu.CompilerParams(
            collective_id=0, has_side_effects=True, vmem_limit_bytes=58 * 1024 * 1024
        ),
    )(queries, kv_prev, hidden_in, norm_gain.reshape(1, model), w_out, w_kv.transpose(1, 0, 2))


def attend_gathered(query_heads, key_value, row_start):
    row_count, head_count = query_heads.shape[:2]
    incoming = lax.all_gather(key_value, "ctx", axis=0, tiled=True)
    block_rows = incoming.shape[0]
    key_block = incoming[:, 0].reshape(block_rows, head_count, HD)
    value_block = incoming[:, 1].reshape(block_rows, head_count, HD)
    scores = (
        jnp.einsum("qhd,khd->qhk", query_heads, key_block, preferred_element_type=jnp.float32)
        * HD ** (-0.5)
    )
    positions = row_start + jnp.arange(row_count)
    allowed = (positions[:, None] >= jnp.arange(block_rows)[None, :])[:, None, :]
    scores = jnp.where(allowed, scores, MASKED)
    weights = jnp.where(allowed, jnp.exp(scores - jnp.max(scores, axis=2, keepdims=True)), 0.0)
    row_sum = jnp.sum(weights, axis=2)
    weighted = jnp.einsum(
        "qhk,khd->qhd", weights.astype(jnp.bfloat16), value_block, preferred_element_type=jnp.float32
    )
    return (weighted / row_sum[:, :, None]).astype(jnp.bfloat16).reshape(row_count, head_count * HD)


def gathered_device(hidden_in, queries, kv_prev, norm_gain, w_kv, w_out):
    row_count, local_width = queries.shape
    head_count = local_width // HD
    row_start = lax.axis_index("ctx") * row_count
    column_start = lax.axis_index("head") * local_width
    out_rows = lax.all_gather(w_out, "ctx", axis=1, tiled=True)
    kv_weights = w_kv.reshape(w_kv.shape[0], 2 * local_width)
    gain_all = norm_gain.astype(jnp.float32)
    query_heads = queries.reshape(row_count, head_count, HD)
    input_all = lax.all_gather(hidden_in, "head", axis=1, tiled=True).astype(jnp.float32)
    key_value = kv_prev
    for _ in range(ITERS):
        attended = attend_gathered(query_heads, key_value, row_start)
        partial_value = jnp.dot(attended, out_rows, preferred_element_type=jnp.float32)
        branch_sum = lax.psum(partial_value.astype(jnp.bfloat16), "head").astype(jnp.float32)
        hidden = input_all + branch_sum
        mean_square = jnp.mean(hidden * hidden, axis=1, keepdims=True)
        normed = (hidden * lax.rsqrt(mean_square + EPSILON) * gain_all).astype(jnp.bfloat16)
        fresh_kv = jnp.dot(normed, kv_weights, preferred_element_type=jnp.float32)
        hidden_out = lax.dynamic_slice_in_dim(hidden, column_start, local_width, 1)
        kv_product = fresh_kv.reshape(row_count, 2, local_width)
        key_value = kv_product.astype(jnp.bfloat16)
    return (hidden_out, kv_product)


def per_device(n, zn, *args):
    rows, width = args[1].shape
    if width == n * HD and n % CORES == 0 and rows % (16 * zn) == 0 and zn > 1:
        return fused_device(n, zn, *args)
    return gathered_device(*args)


def solution(mesh):
    in_specs = (
        P("ctx", "head"),
        P("ctx", "head"),
        P("ctx", None, "head"),
        P(),
        P(None, None, "head"),
        P("head", "ctx"),
    )
    out_specs = (P("ctx", "head"), P("ctx", None, "head"))
    return jax.shard_map(
        functools.partial(per_device, mesh.shape["ctx"], mesh.shape["head"]),
        mesh=mesh, in_specs=in_specs, out_specs=out_specs, check_vma=False,
    )
```

```python
import functools

import jax
import jax.numpy as jnp
from jax import lax
from jax.experimental import pallas as pl
from jax.experimental.pallas import tpu as pltpu
from jax.sharding import PartitionSpec as P

HD = 128
ITERS = 2
CORES = 2

MASKED = -1e30
EPSILON = 1e-05
MESH = pl.DeviceIdType.MESH


def attend_block(query, keys, values, row_start):
    scores = lax.dot_general(
        query, keys, (((1,), (1,)), ((), ())), preferred_element_type=jnp.float32
    ) * (HD ** (-0.5))
    rows = row_start + lax.broadcasted_iota(jnp.int32, scores.shape, 0)
    columns = lax.broadcasted_iota(jnp.int32, scores.shape, 1)
    scores = jnp.where(rows >= columns, scores, MASKED)
    weights = jnp.exp(scores - jnp.max(scores, axis=1, keepdims=True))
    row_sum = jnp.sum(weights, axis=1, keepdims=True)
    weighted = jnp.dot(weights.astype(jnp.bfloat16), values, preferred_element_type=jnp.float32)
    return (weighted / row_sum).astype(jnp.bfloat16)


def fused_kernel(
    n, zn, q_ref, kv_ref, hin_ref, gain_ref, wout_ref, wkv_hbm, hid_ref, kvo_ref,
    q_all, kv_land, kv_all, w_pair, hin_all, a_send, a_all, p_send, rs, acc, b_send, b_all, scaled, squares, kv_acc, kv_send, kv_back, wkv, staged,
    load_sem, local_sem, pair_send, pair_recv, in_send, in_recv, hin_send, hin_recv,
    a_ssem, a_rsem, p_ssem, p_rsem, b_ssem, b_rsem, g_ssem, g_rsem, kv_ssem, kv_rsem, x_ssem, x_rsem, y_ssem, y_rsem,
):
    c = lax.axis_index("ctx")
    z = lax.axis_index("head")
    core = lax.rem(c, CORES)
    k = lax.div(c, CORES)
    groups = n // CORES
    rows, width = q_ref.shape
    quarter = rows // zn
    block = rows * CORES
    chip_width = CORES * wout_ref.shape[1]
    pending = []

    def remote(src, dst, ssem, rsem, where):
        return pltpu.make_async_remote_copy(
            src_ref=src, dst_ref=dst, send_sem=ssem, recv_sem=rsem, device_id=where, device_id_type=MESH
        )

    def send(*args):
        copy = remote(*args)
        copy.start()
        pending.append((None, copy))
        return copy

    def send_if(condition, copy):
        pl.when(condition)(copy.start)
        pending.append((condition, copy))

    def cols(index, size):
        return pl.ds(pl.multiple_of(index * size, size), size)

    chunk = staged.shape[1]
    chunk_count = wkv_hbm.shape[0] // chunk
    sibling = {"ctx": k * CORES + 1 - core}

    def load(j):
        slot = lax.rem(j, 2)
        return pltpu.make_async_copy(wkv_hbm.at[cols(j, chunk)], staged.at[slot], load_sem.at[slot])

    def part_weights(first, last):
        @pl.loop(first, last)
        def _(j):
            load(j).wait()
            for kind in range(CORES):
                @pl.when(core == kind)
                def _():
                    wkv[cols(j, chunk), :] = staged[lax.rem(j, 2), :, kind, :]

            @pl.when(j + 2 < chunk_count)
            def _():
                load(j + 2).start()

    load(jnp.int32(0)).start()
    load(jnp.int32(1)).start()
    own_w = pltpu.make_async_copy(wout_ref, w_pair.at[core], local_sem)
    own_w.start()

    barrier = pltpu.get_barrier_semaphore()
    for d in range(1, n):
        pl.semaphore_signal(barrier, inc=1, device_id={"ctx": lax.rem(c + d, n)}, device_id_type=MESH)
    for d in range(1, zn):
        pl.semaphore_signal(barrier, inc=1, device_id={"head": lax.rem(z + d, zn)}, device_id_type=MESH)
    pl.semaphore_wait(barrier, n - 1 + zn - 1)

    arrivals = []
    for d in range(1, n):
        peer = lax.rem(c + d, n)
        arrivals.append((None, send(
            kv_ref.at[:, :, cols(peer, HD)], kv_land.at[cols(c, rows)],
            in_send.at[0, d], in_recv.at[0, d], {"ctx": peer},
        )))
        arrivals.append((None, send(
            q_ref.at[:, cols(peer, HD)], q_all.at[cols(c, rows)],
            in_send.at[1, d], in_recv.at[1, d], {"ctx": peer},
        )))
    kv_land[cols(c, rows), :, :] = kv_ref[:, :, cols(c, HD)]
    q_all[cols(c, rows), :] = q_ref[:, cols(c, HD)]
    pair = send(wout_ref, w_pair.at[core], pair_send, pair_recv, sibling)
    hin_copies = [
        send(hin_ref, hin_all.at[core, :, cols(z, width)], hin_send.at[d], hin_recv.at[d],
             {"head": lax.rem(z + d, zn)})
        for d in range(1, zn)
    ]
    hin_all[core, :, cols(z, width)] = hin_ref[...]

    plan = [chunk_count * part // 16 for part in (0, 6, 11, 12, 13, 14, 16)]
    part_weights(plan[0], plan[1])
    for it in range(ITERS):
        for condition, copy in arrivals:
            if condition is None:
                copy.wait_recv()
            else:
                pl.when(condition)(copy.wait_recv)
        if it == 0:
            for kind in range(2):
                kv_all[it, kind] = kv_land[:, kind, :]

        for i in range(groups):
            limit = (i + 1) * block
            attended = attend_block(
                q_all[i * block:limit, :], kv_all[it, 0, 0:limit, :], kv_all[it, 1, 0:limit, :], i * block
            )
            for side in range(CORES):
                a_send[it, i, side] = attended[side * rows:(side + 1) * rows, :]
        for t in range(groups):
            for d in range(1, n):
                peer = lax.rem(c + d, n)
                i = lax.rem(lax.div(peer, CORES) + 1 + t, groups)
                send(
                    a_send.at[it, i, lax.rem(peer, CORES)], a_all.at[it, i, :, cols(c, HD)],
                    a_ssem.at[it, t, d], a_rsem.at[it, t, d], {"ctx": peer},
                )
        for i in range(groups):
            a_all[it, i, :, cols(c, HD)] = a_send[it, i, core]
        if it == 0:
            part_weights(plan[1], plan[2])
            own_w.wait()
            pair.wait_recv()

        def project(t):
            i = lax.rem(k + 1 + t, groups)
            half = chip_width // CORES
            for d in range(1, n):
                remote(
                    a_send.at[it, i, core], a_all.at[it, i, :, cols(c, HD)],
                    a_ssem.at[it, t, d], a_rsem.at[it, t, d], {"ctx": lax.rem(c + d, n)},
                ).wait_recv()
            for side in range(CORES):
                product = jnp.dot(
                    a_all[it, i], w_pair[side], preferred_element_type=jnp.float32
                ).astype(jnp.bfloat16)
                for s in range(zn):
                    p_send[it, t, s, :, side * half:(side + 1) * half] = product[s * quarter:(s + 1) * quarter, :]

        def step_copy(t, s, way):
            return remote(
                p_send.at[it, t, s], rs.at[it, way, t, s], p_ssem.at[it, way, t, s], p_rsem.at[it, way, t, s],
                {"head": z + 1 if way == 0 else z - 1},
            )

        def pass_sums(t, hop):
            for way in range(2):
                @pl.when(z == (hop if way == 0 else zn - 1 - hop))
                def _():
                    for j in range(zn - 1 - hop, 0, -1):
                        s = hop + j if way == 0 else zn - 1 - hop - j
                        copy = step_copy(t, s, way)
                        if hop > 0:
                            copy.wait_recv()
                            p_send[it, t, s] = (
                                p_send[it, t, s].astype(jnp.float32) + rs[it, way, t, s].astype(jnp.float32)
                            ).astype(jnp.bfloat16)
                        copy.start()

                for j in range(zn - 1 - hop, 0, -1):
                    s = hop + j if way == 0 else zn - 1 - hop - j
                    pending.append((z == (hop if way == 0 else zn - 1 - hop), step_copy(t, s, way)))

        def finish_sums(t):
            acc[...] = p_send[it, t, z].astype(jnp.float32)
            for way in range(2):
                @pl.when(z > 0 if way == 0 else z < zn - 1)
                def _():
                    step_copy(t, z, way).wait_recv()
                    acc[...] += rs[it, way, t, z].astype(jnp.float32)
            i = lax.rem(k + 1 + t, groups)
            if t == groups - 1:
                b_all[it, core, z, :, cols(k, chip_width)] = acc[...].astype(jnp.bfloat16)
            else:
                b_send[it, t] = acc[...].astype(jnp.bfloat16)
                b_copies.append(send(
                    b_send.at[it, t], b_all.at[it, core, z, :, cols(k, chip_width)],
                    b_ssem.at[it, t], b_rsem.at[it, t], {"ctx": i * CORES + core},
                ))

        def piece_copy(t, s, way):
            place = b_all.at[it, core, s, :, cols(lax.rem(k + groups - 1 - t, groups), chip_width)]
            return remote(
                place, place, g_ssem.at[it, way, t, s], g_rsem.at[it, way, t, s],
                {"head": z + 1 if way == 0 else z - 1},
            )

        def pair_copy(t, s, side):
            place = b_all.at[it, side, s, :, cols(lax.rem(k + groups - 1 - t, groups), chip_width)]
            return remote(place, place, x_ssem.at[it, t, s], x_rsem.at[it, t, s], sibling)

        def start_piece(t):
            if t < groups - 1:
                b_copies[t].wait_recv()
            send_if(z >= 0, pair_copy(t, z, core))
            send_if(z < zn - 1, piece_copy(t, z, 0))
            send_if(z > 0, piece_copy(t, z, 1))

        def pass_pieces(t, j):
            for way in range(2):
                s = z - j if way == 0 else z + j
                there = s >= 0 if way == 0 else s < zn
                ahead = z < zn - 1 if way == 0 else z > 0
                copy = piece_copy(t, s, way)
                pl.when(there)(copy.wait_recv)
                send_if(there & ahead, copy)
                send_if(there, pair_copy(t, s, core))

        def consume(t):
            place = cols(lax.rem(k + groups - 1 - t, groups), chip_width)
            for part in range(zn):
                pair_copy(t, part, 1 - core).wait_recv()
            both = CORES * rows
            hidden = hin_all[:, :, place].astype(jnp.float32).reshape(both, chip_width) + b_all[
                it, :, :, :, place
            ].astype(jnp.float32).reshape(both, chip_width)
            square = jnp.sum(hidden * hidden, axis=1, keepdims=True)
            scaled[...] = (hidden * gain_ref[:, place].astype(jnp.float32)).astype(jnp.bfloat16)
            squares[...] = square if t == 0 else squares[...] + square
            scale = lax.rsqrt(squares[...] / hin_all.shape[2] + EPSILON)

            @pl.loop(0, width // 256)
            def _(j):
                product = jnp.dot(
                    scaled[...], wkv[place, cols(j, 256)], preferred_element_type=jnp.float32
                )
                if t > 0:
                    product = product + kv_acc[:, cols(j, 256)]
                if t == groups - 1:
                    product = product * scale
                if t == groups - 1 and it < ITERS - 1:
                    kv_send[:, cols(j, 256)] = product.astype(jnp.bfloat16)
                else:
                    kv_acc[:, cols(j, 256)] = product

            if t < groups - 1:
                return []
            if it < ITERS - 1:
                copies = []
                for d in range(1, n):
                    peer = lax.rem(c + d, n)
                    send(
                        kv_send.at[:, cols(peer, HD)], kv_all.at[it + 1, core, cols(k, both)],
                        kv_ssem.at[d], kv_rsem.at[core, k], {"ctx": peer},
                    )
                kv_all[it + 1, core, cols(k, both), :] = kv_send[:, cols(c, HD)]
                for kind in range(CORES):
                    for chip in range(groups):
                        copies.append(((core != kind) | (k != chip), remote(
                            kv_send.at[:, cols(c, HD)], kv_all.at[it + 1, kind, cols(chip, both)],
                            kv_ssem.at[0], kv_rsem.at[kind, chip], sibling,
                        )))
                return copies
            back = send(kv_acc.at[cols(1 - core, rows)], kv_back, y_ssem, y_rsem, sibling)
            for kind in range(CORES):
                @pl.when(core == kind)
                def _():
                    kvo_ref[:, kind, :] = kv_acc[kind * rows:(kind + 1) * rows, :]
            back.wait_recv()
            for kind in range(CORES):
                @pl.when(core == kind)
                def _():
                    kvo_ref[:, 1 - kind, :] = kv_back[...]
            return []

        b_copies = []
        tasks = [project]
        tasks += [functools.partial(pass_sums, hop=hop) for hop in range(zn - 1)]
        tasks += [finish_sums, start_piece]
        tasks += [functools.partial(pass_pieces, j=j) for j in range(1, zn)]
        lags = [0] + list(range(zn - 1)) + list(range(zn - 1, 2 * zn))
        for stage in range(groups + 2 * zn):
            for task, lag in zip(tasks, lags):
                if 0 <= stage - lag < groups:
                    task(stage - lag)
            if it == 0 and stage < groups:
                part_weights(plan[2 + stage], plan[3 + stage])
            if it == 0 and stage == groups:
                for copy in hin_copies:
                    copy.wait_recv()
                hin_pair = send(hin_all.at[core], hin_all.at[core], hin_send.at[0], hin_recv.at[0], sibling)
            if it == 0 and stage == 2 * zn:
                hin_pair.wait_recv()
            if 0 <= stage - 2 * zn < groups - 1:
                consume(stage - 2 * zn)
        arrivals = consume(groups - 1)
        if it == ITERS - 1:
            hid_ref[...] = hin_ref[...].astype(jnp.float32) + b_all[it, core, :, :, cols(z, width)].astype(
                jnp.float32
            ).reshape(rows, width)

    for condition, copy in pending:
        if condition is None:
            copy.wait_send()
        else:
            pl.when(condition)(copy.wait_send)


def fused_device(n, zn, hidden_in, queries, kv_prev, norm_gain, w_kv, w_out):
    rows, width = queries.shape
    model = w_kv.shape[0]
    tokens = rows * n
    groups = n // CORES
    quarter = rows // zn
    chip_width = CORES * w_out.shape[1]
    vmem = pl.BlockSpec(memory_space=pltpu.VMEM)
    bf16 = jnp.bfloat16
    dma = pltpu.SemaphoreType.DMA
    return pl.pallas_call(
        functools.partial(fused_kernel, n, zn),
        out_shape=(
            jax.ShapeDtypeStruct((rows, width), jnp.float32),
            jax.ShapeDtypeStruct((rows, 2, width), jnp.float32),
        ),
        in_specs=[vmem] * 5 + [pl.BlockSpec(memory_space=pl.ANY)],
        out_specs=(vmem, vmem),
        scratch_shapes=[
            pltpu.VMEM((tokens, HD), bf16),
            pltpu.VMEM((tokens, 2, HD), bf16),
            pltpu.VMEM((ITERS, 2, tokens, HD), bf16),
            pltpu.VMEM((CORES,) + w_out.shape, bf16),
            pltpu.VMEM((CORES, rows, model), bf16),
            pltpu.VMEM((ITERS, groups, CORES, rows, HD), bf16),
            pltpu.VMEM((ITERS, groups, rows, width), bf16),
            pltpu.VMEM((ITERS, groups, zn, quarter, chip_width), bf16),
            pltpu.VMEM((ITERS, 2, groups, zn, quarter, chip_width), bf16),
            pltpu.VMEM((quarter, chip_width), jnp.float32),
            pltpu.VMEM((ITERS, groups - 1, quarter, chip_width), bf16),
            pltpu.VMEM((ITERS, CORES, zn, quarter, model), bf16),
            pltpu.VMEM((CORES * rows, chip_width), bf16),
            pltpu.VMEM((CORES * rows, 1), jnp.float32),
            pltpu.VMEM((CORES * rows, width), jnp.float32),
            pltpu.VMEM((CORES * rows, width), bf16),
            pltpu.VMEM((rows, width), jnp.float32),
            pltpu.VMEM((model, width), bf16),
            pltpu.VMEM((2, 64, 2, width), bf16),
            dma((2,)), dma, dma, dma,
            dma((2, n)), dma((2, n)),
            dma((zn,)), dma((zn,)),
            dma((ITERS, groups, n)), dma((ITERS, groups, n)),
            dma((ITERS, 2, groups, zn)), dma((ITERS, 2, groups, zn)),
            dma((ITERS, groups)), dma((ITERS, groups)),
            dma((ITERS, 2, groups, zn)), dma((ITERS, 2, groups, zn)),
            dma((n,)), dma((CORES, groups)),
            dma((ITERS, groups, zn)), dma((ITERS, groups, zn)),
            dma, dma,
        ],
        compiler_params=pltpu.CompilerParams(
            collective_id=0, has_side_effects=True, vmem_limit_bytes=58 * 1024 * 1024
        ),
    )(queries, kv_prev, hidden_in, norm_gain.reshape(1, model), w_out, w_kv)


def attend_gathered(query_heads, key_value, row_start):
    row_count, head_count = query_heads.shape[:2]
    incoming = lax.all_gather(key_value, "ctx", axis=0, tiled=True)
    block_rows = incoming.shape[0]
    key_block = incoming[:, 0].reshape(block_rows, head_count, HD)
    value_block = incoming[:, 1].reshape(block_rows, head_count, HD)
    scores = (
        jnp.einsum("qhd,khd->qhk", query_heads, key_block, preferred_element_type=jnp.float32)
        * HD ** (-0.5)
    )
    positions = row_start + jnp.arange(row_count)
    allowed = (positions[:, None] >= jnp.arange(block_rows)[None, :])[:, None, :]
    scores = jnp.where(allowed, scores, MASKED)
    weights = jnp.where(allowed, jnp.exp(scores - jnp.max(scores, axis=2, keepdims=True)), 0.0)
    row_sum = jnp.sum(weights, axis=2)
    weighted = jnp.einsum(
        "qhk,khd->qhd", weights.astype(jnp.bfloat16), value_block, preferred_element_type=jnp.float32
    )
    return (weighted / row_sum[:, :, None]).astype(jnp.bfloat16).reshape(row_count, head_count * HD)


def gathered_device(hidden_in, queries, kv_prev, norm_gain, w_kv, w_out):
    row_count, local_width = queries.shape
    head_count = local_width // HD
    row_start = lax.axis_index("ctx") * row_count
    column_start = lax.axis_index("head") * local_width
    out_rows = lax.all_gather(w_out, "ctx", axis=1, tiled=True)
    kv_weights = w_kv.reshape(w_kv.shape[0], 2 * local_width)
    gain_all = norm_gain.astype(jnp.float32)
    query_heads = queries.reshape(row_count, head_count, HD)
    input_all = lax.all_gather(hidden_in, "head", axis=1, tiled=True).astype(jnp.float32)
    key_value = kv_prev
    for _ in range(ITERS):
        attended = attend_gathered(query_heads, key_value, row_start)
        partial_value = jnp.dot(attended, out_rows, preferred_element_type=jnp.float32)
        branch_sum = lax.psum(partial_value.astype(jnp.bfloat16), "head").astype(jnp.float32)
        hidden = input_all + branch_sum
        mean_square = jnp.mean(hidden * hidden, axis=1, keepdims=True)
        normed = (hidden * lax.rsqrt(mean_square + EPSILON) * gain_all).astype(jnp.bfloat16)
        fresh_kv = jnp.dot(normed, kv_weights, preferred_element_type=jnp.float32)
        hidden_out = lax.dynamic_slice_in_dim(hidden, column_start, local_width, 1)
        kv_product = fresh_kv.reshape(row_count, 2, local_width)
        key_value = kv_product.astype(jnp.bfloat16)
    return (hidden_out, kv_product)


def per_device(n, zn, *args):
    rows, width = args[1].shape
    if width == n * HD and n % CORES == 0 and rows % (16 * zn) == 0 and zn > 1:
        return fused_device(n, zn, *args)
    return gathered_device(*args)


def solution(mesh):
    in_specs = (
        P("ctx", "head"),
        P("ctx", "head"),
        P("ctx", None, "head"),
        P(),
        P(None, None, "head"),
        P("head", "ctx"),
    )
    out_specs = (P("ctx", "head"), P("ctx", None, "head"))
    return jax.shard_map(
        functools.partial(per_device, mesh.shape["ctx"], mesh.shape["head"]),
        mesh=mesh, in_specs=in_specs, out_specs=out_specs, check_vma=False,
    )
```

```python
import functools

import jax
import jax.numpy as jnp
from jax import lax
from jax.experimental import pallas as pl
from jax.experimental.pallas import tpu as pltpu
from jax.sharding import PartitionSpec as P

HD = 128
ITERS = 2
CORES = 2

MASKED = -1e30
EPSILON = 1e-05
MESH = pl.DeviceIdType.MESH


def attend_block(query, keys, values, row_start):
    scores = lax.dot_general(
        query, keys, (((1,), (1,)), ((), ())), preferred_element_type=jnp.float32
    ) * (HD ** (-0.5))
    rows = row_start + lax.broadcasted_iota(jnp.int32, scores.shape, 0)
    columns = lax.broadcasted_iota(jnp.int32, scores.shape, 1)
    scores = jnp.where(rows >= columns, scores, MASKED)
    weights = jnp.exp(scores - jnp.max(scores, axis=1, keepdims=True))
    row_sum = jnp.sum(weights, axis=1, keepdims=True)
    weighted = jnp.dot(weights.astype(jnp.bfloat16), values, preferred_element_type=jnp.float32)
    return (weighted / row_sum).astype(jnp.bfloat16)


def fused_kernel(
    n, zn, q_ref, kv_ref, hin_ref, gain_ref, wout_ref, wkv_hbm, hid_ref, kvo_ref,
    q_all, kv_land, kv_all, w_pair, hin_all, a_send, a_all, p_send, rs, acc, b_send, b_all, scaled, squares, kv_acc, kv_send, kv_back, wkv, staged,
    load_sem, local_sem, pair_send, pair_recv, in_send, in_recv, hin_send, hin_recv,
    a_ssem, a_rsem, p_ssem, p_rsem, b_ssem, b_rsem, g_ssem, g_rsem, kv_ssem, kv_rsem, x_ssem, x_rsem, y_ssem, y_rsem,
):
    c = lax.axis_index("ctx")
    z = lax.axis_index("head")
    core = lax.rem(c, CORES)
    k = lax.div(c, CORES)
    groups = n // CORES
    rows, width = q_ref.shape
    quarter = rows // zn
    block = rows * CORES
    chip_width = CORES * wout_ref.shape[1]
    pending = []

    def remote(src, dst, ssem, rsem, where):
        return pltpu.make_async_remote_copy(
            src_ref=src, dst_ref=dst, send_sem=ssem, recv_sem=rsem, device_id=where, device_id_type=MESH
        )

    def send(*args):
        copy = remote(*args)
        copy.start()
        pending.append((None, copy))
        return copy

    def send_if(condition, copy):
        pl.when(condition)(copy.start)
        pending.append((condition, copy))

    def cols(index, size):
        return pl.ds(pl.multiple_of(index * size, size), size)

    chunk = staged.shape[1]
    chunk_count = wkv_hbm.shape[0] // chunk
    sibling = {"ctx": k * CORES + 1 - core}

    def span_of(j):
        each = chip_width // chunk
        first = lax.rem(k + groups - 1 - lax.div(j, each), groups)
        return cols(lax.rem(first + groups, groups) * each + lax.rem(j, each), chunk)

    def load(j):
        slot = lax.rem(j, 2)
        return pltpu.make_async_copy(wkv_hbm.at[span_of(j)], staged.at[slot], load_sem.at[slot])

    def part_weights(first, last):
        @pl.loop(first, last)
        def _(j):
            load(j).wait()
            for kind in range(CORES):
                @pl.when(core == kind)
                def _():
                    wkv[span_of(j), :] = staged[lax.rem(j, 2), :, kind, :]

            @pl.when(j + 2 < chunk_count)
            def _():
                load(j + 2).start()

    load(jnp.int32(0)).start()
    load(jnp.int32(1)).start()
    own_w = pltpu.make_async_copy(wout_ref, w_pair.at[core], local_sem)
    own_w.start()

    barrier = pltpu.get_barrier_semaphore()
    for d in range(1, n):
        pl.semaphore_signal(barrier, inc=1, device_id={"ctx": lax.rem(c + d, n)}, device_id_type=MESH)
    for d in range(1, zn):
        pl.semaphore_signal(barrier, inc=1, device_id={"head": lax.rem(z + d, zn)}, device_id_type=MESH)
    pl.semaphore_wait(barrier, n - 1 + zn - 1)

    arrivals = []
    for d in range(1, n):
        peer = lax.rem(c + d, n)
        arrivals.append((None, send(
            kv_ref.at[:, :, cols(peer, HD)], kv_land.at[cols(c, rows)],
            in_send.at[0, d], in_recv.at[0, d], {"ctx": peer},
        )))
        arrivals.append((None, send(
            q_ref.at[:, cols(peer, HD)], q_all.at[cols(c, rows)],
            in_send.at[1, d], in_recv.at[1, d], {"ctx": peer},
        )))
    kv_land[cols(c, rows), :, :] = kv_ref[:, :, cols(c, HD)]
    q_all[cols(c, rows), :] = q_ref[:, cols(c, HD)]
    pair = send(wout_ref, w_pair.at[core], pair_send, pair_recv, sibling)
    hin_copies = [
        send(hin_ref, hin_all.at[core, :, cols(z, width)], hin_send.at[d], hin_recv.at[d],
             {"head": lax.rem(z + d, zn)})
        for d in range(1, zn)
    ]
    hin_all[core, :, cols(z, width)] = hin_ref[...]

    plan = [chunk_count * part // 64 for part in (0, 12, 16, 18, 20, 22, 24, 28, 32, 36, 40, 46, 54, 64)]
    part_weights(plan[0], plan[1])
    for it in range(ITERS):
        for condition, copy in arrivals:
            if condition is None:
                copy.wait_recv()
            else:
                pl.when(condition)(copy.wait_recv)
        if it == 0:
            for kind in range(2):
                kv_all[it, kind] = kv_land[:, kind, :]

        for i in range(groups):
            limit = (i + 1) * block
            attended = attend_block(
                q_all[i * block:limit, :], kv_all[it, 0, 0:limit, :], kv_all[it, 1, 0:limit, :], i * block
            )
            for side in range(CORES):
                a_send[it, i, side] = attended[side * rows:(side + 1) * rows, :]
        for t in range(groups):
            for d in range(1, n):
                peer = lax.rem(c + d, n)
                i = lax.rem(lax.div(peer, CORES) + 1 + t, groups)
                send(
                    a_send.at[it, i, lax.rem(peer, CORES)], a_all.at[it, i, :, cols(c, HD)],
                    a_ssem.at[it, t, d], a_rsem.at[it, t, d], {"ctx": peer},
                )
        for i in range(groups):
            a_all[it, i, :, cols(c, HD)] = a_send[it, i, core]
        if it == 0:
            part_weights(plan[1], plan[2])
            own_w.wait()
            pair.wait_recv()

        def project(t):
            i = lax.rem(k + 1 + t, groups)
            half = chip_width // CORES
            for d in range(1, n):
                remote(
                    a_send.at[it, i, core], a_all.at[it, i, :, cols(c, HD)],
                    a_ssem.at[it, t, d], a_rsem.at[it, t, d], {"ctx": lax.rem(c + d, n)},
                ).wait_recv()
            for side in range(CORES):
                product = jnp.dot(
                    a_all[it, i], w_pair[side], preferred_element_type=jnp.float32
                ).astype(jnp.bfloat16)
                for s in range(zn):
                    p_send[it, t, s, :, side * half:(side + 1) * half] = product[s * quarter:(s + 1) * quarter, :]

        def step_copy(t, s, way):
            return remote(
                p_send.at[it, t, s], rs.at[it, way, t, s], p_ssem.at[it, way, t, s], p_rsem.at[it, way, t, s],
                {"head": z + 1 if way == 0 else z - 1},
            )

        def pass_sums(t, hop):
            for way in range(2):
                @pl.when(z == (hop if way == 0 else zn - 1 - hop))
                def _():
                    for j in range(zn - 1 - hop, 0, -1):
                        s = hop + j if way == 0 else zn - 1 - hop - j
                        copy = step_copy(t, s, way)
                        if hop > 0:
                            copy.wait_recv()
                            p_send[it, t, s] = (
                                p_send[it, t, s].astype(jnp.float32) + rs[it, way, t, s].astype(jnp.float32)
                            ).astype(jnp.bfloat16)
                        copy.start()

                for j in range(zn - 1 - hop, 0, -1):
                    s = hop + j if way == 0 else zn - 1 - hop - j
                    pending.append((z == (hop if way == 0 else zn - 1 - hop), step_copy(t, s, way)))

        def finish_sums(t):
            acc[...] = p_send[it, t, z].astype(jnp.float32)
            for way in range(2):
                @pl.when(z > 0 if way == 0 else z < zn - 1)
                def _():
                    step_copy(t, z, way).wait_recv()
                    acc[...] += rs[it, way, t, z].astype(jnp.float32)
            i = lax.rem(k + 1 + t, groups)
            if t == groups - 1:
                b_all[it, core, z, :, cols(k, chip_width)] = acc[...].astype(jnp.bfloat16)
            else:
                b_send[it, t] = acc[...].astype(jnp.bfloat16)
                b_copies.append(send(
                    b_send.at[it, t], b_all.at[it, core, z, :, cols(k, chip_width)],
                    b_ssem.at[it, t], b_rsem.at[it, t], {"ctx": i * CORES + core},
                ))

        def piece_copy(t, s, way):
            place = b_all.at[it, core, s, :, cols(lax.rem(k + groups - 1 - t, groups), chip_width)]
            return remote(
                place, place, g_ssem.at[it, way, t, s], g_rsem.at[it, way, t, s],
                {"head": z + 1 if way == 0 else z - 1},
            )

        def pair_copy(t, s, side):
            place = b_all.at[it, side, s, :, cols(lax.rem(k + groups - 1 - t, groups), chip_width)]
            return remote(place, place, x_ssem.at[it, t, s], x_rsem.at[it, t, s], sibling)

        def start_piece(t):
            if t < groups - 1:
                b_copies[t].wait_recv()
            send_if(z >= 0, pair_copy(t, z, core))
            send_if(z < zn - 1, piece_copy(t, z, 0))
            send_if(z > 0, piece_copy(t, z, 1))

        def pass_pieces(t, j):
            for way in range(2):
                s = z - j if way == 0 else z + j
                there = s >= 0 if way == 0 else s < zn
                ahead = z < zn - 1 if way == 0 else z > 0
                copy = piece_copy(t, s, way)
                pl.when(there)(copy.wait_recv)
                send_if(there & ahead, copy)
                send_if(there, pair_copy(t, s, core))

        def consume(t):
            place = cols(lax.rem(k + groups - 1 - t, groups), chip_width)
            for part in range(zn):
                pair_copy(t, part, 1 - core).wait_recv()
            both = CORES * rows
            hidden = hin_all[:, :, place].astype(jnp.float32).reshape(both, chip_width) + b_all[
                it, :, :, :, place
            ].astype(jnp.float32).reshape(both, chip_width)
            square = jnp.sum(hidden * hidden, axis=1, keepdims=True)
            scaled[...] = (hidden * gain_ref[:, place].astype(jnp.float32)).astype(jnp.bfloat16)
            squares[...] = square if t == 0 else squares[...] + square
            scale = lax.rsqrt(squares[...] / hin_all.shape[2] + EPSILON)

            @pl.loop(0, width // 256)
            def _(j):
                product = jnp.dot(
                    scaled[...], wkv[place, cols(j, 256)], preferred_element_type=jnp.float32
                )
                if t > 0:
                    product = product + kv_acc[:, cols(j, 256)]
                if t == groups - 1:
                    product = product * scale
                if t == groups - 1 and it < ITERS - 1:
                    kv_send[:, cols(j, 256)] = product.astype(jnp.bfloat16)
                else:
                    kv_acc[:, cols(j, 256)] = product

            if t < groups - 1:
                return []
            if it < ITERS - 1:
                copies = []
                for d in range(1, n):
                    peer = lax.rem(c + d, n)
                    send(
                        kv_send.at[:, cols(peer, HD)], kv_all.at[it + 1, core, cols(k, both)],
                        kv_ssem.at[d], kv_rsem.at[core, k], {"ctx": peer},
                    )
                kv_all[it + 1, core, cols(k, both), :] = kv_send[:, cols(c, HD)]
                for kind in range(CORES):
                    for chip in range(groups):
                        copies.append(((core != kind) | (k != chip), remote(
                            kv_send.at[:, cols(c, HD)], kv_all.at[it + 1, kind, cols(chip, both)],
                            kv_ssem.at[0], kv_rsem.at[kind, chip], sibling,
                        )))
                return copies
            back = send(kv_acc.at[cols(1 - core, rows)], kv_back, y_ssem, y_rsem, sibling)
            for kind in range(CORES):
                @pl.when(core == kind)
                def _():
                    kvo_ref[:, kind, :] = kv_acc[kind * rows:(kind + 1) * rows, :]
            back.wait_recv()
            for kind in range(CORES):
                @pl.when(core == kind)
                def _():
                    kvo_ref[:, 1 - kind, :] = kv_back[...]
            return []

        b_copies = []
        tasks = [project]
        tasks += [functools.partial(pass_sums, hop=hop) for hop in range(zn - 1)]
        tasks += [finish_sums, start_piece]
        tasks += [functools.partial(pass_pieces, j=j) for j in range(1, zn)]
        lags = [0] + list(range(zn - 1)) + list(range(zn - 1, 2 * zn))
        for stage in range(groups + 2 * zn):
            for task, lag in zip(tasks, lags):
                if 0 <= stage - lag < groups:
                    task(stage - lag)
            if it == 0 and stage + 3 < len(plan):
                part_weights(plan[2 + stage], plan[3 + stage])
            if it == 0 and stage == groups:
                for copy in hin_copies:
                    copy.wait_recv()
                hin_pair = send(hin_all.at[core], hin_all.at[core], hin_send.at[0], hin_recv.at[0], sibling)
            if it == 0 and stage == 2 * zn:
                hin_pair.wait_recv()
            if 0 <= stage - 2 * zn < groups - 1:
                consume(stage - 2 * zn)
        arrivals = consume(groups - 1)
        if it == ITERS - 1:
            hid_ref[...] = hin_ref[...].astype(jnp.float32) + b_all[it, core, :, :, cols(z, width)].astype(
                jnp.float32
            ).reshape(rows, width)

    for condition, copy in pending:
        if condition is None:
            copy.wait_send()
        else:
            pl.when(condition)(copy.wait_send)


def fused_device(n, zn, hidden_in, queries, kv_prev, norm_gain, w_kv, w_out):
    rows, width = queries.shape
    model = w_kv.shape[0]
    tokens = rows * n
    groups = n // CORES
    quarter = rows // zn
    chip_width = CORES * w_out.shape[1]
    vmem = pl.BlockSpec(memory_space=pltpu.VMEM)
    bf16 = jnp.bfloat16
    dma = pltpu.SemaphoreType.DMA
    return pl.pallas_call(
        functools.partial(fused_kernel, n, zn),
        out_shape=(
            jax.ShapeDtypeStruct((rows, width), jnp.float32),
            jax.ShapeDtypeStruct((rows, 2, width), jnp.float32),
        ),
        in_specs=[vmem] * 5 + [pl.BlockSpec(memory_space=pl.ANY)],
        out_specs=(vmem, vmem),
        scratch_shapes=[
            pltpu.VMEM((tokens, HD), bf16),
            pltpu.VMEM((tokens, 2, HD), bf16),
            pltpu.VMEM((ITERS, 2, tokens, HD), bf16),
            pltpu.VMEM((CORES,) + w_out.shape, bf16),
            pltpu.VMEM((CORES, rows, model), bf16),
            pltpu.VMEM((ITERS, groups, CORES, rows, HD), bf16),
            pltpu.VMEM((ITERS, groups, rows, width), bf16),
            pltpu.VMEM((ITERS, groups, zn, quarter, chip_width), bf16),
            pltpu.VMEM((ITERS, 2, groups, zn, quarter, chip_width), bf16),
            pltpu.VMEM((quarter, chip_width), jnp.float32),
            pltpu.VMEM((ITERS, groups - 1, quarter, chip_width), bf16),
            pltpu.VMEM((ITERS, CORES, zn, quarter, model), bf16),
            pltpu.VMEM((CORES * rows, chip_width), bf16),
            pltpu.VMEM((CORES * rows, 1), jnp.float32),
            pltpu.VMEM((CORES * rows, width), jnp.float32),
            pltpu.VMEM((CORES * rows, width), bf16),
            pltpu.VMEM((rows, width), jnp.float32),
            pltpu.VMEM((model, width), bf16),
            pltpu.VMEM((2, 64, 2, width), bf16),
            dma((2,)), dma, dma, dma,
            dma((2, n)), dma((2, n)),
            dma((zn,)), dma((zn,)),
            dma((ITERS, groups, n)), dma((ITERS, groups, n)),
            dma((ITERS, 2, groups, zn)), dma((ITERS, 2, groups, zn)),
            dma((ITERS, groups)), dma((ITERS, groups)),
            dma((ITERS, 2, groups, zn)), dma((ITERS, 2, groups, zn)),
            dma((n,)), dma((CORES, groups)),
            dma((ITERS, groups, zn)), dma((ITERS, groups, zn)),
            dma, dma,
        ],
        compiler_params=pltpu.CompilerParams(
            collective_id=0, has_side_effects=True, vmem_limit_bytes=58 * 1024 * 1024
        ),
    )(queries, kv_prev, hidden_in, norm_gain.reshape(1, model), w_out, w_kv)


def attend_gathered(query_heads, key_value, row_start):
    row_count, head_count = query_heads.shape[:2]
    incoming = lax.all_gather(key_value, "ctx", axis=0, tiled=True)
    block_rows = incoming.shape[0]
    key_block = incoming[:, 0].reshape(block_rows, head_count, HD)
    value_block = incoming[:, 1].reshape(block_rows, head_count, HD)
    scores = (
        jnp.einsum("qhd,khd->qhk", query_heads, key_block, preferred_element_type=jnp.float32)
        * HD ** (-0.5)
    )
    positions = row_start + jnp.arange(row_count)
    allowed = (positions[:, None] >= jnp.arange(block_rows)[None, :])[:, None, :]
    scores = jnp.where(allowed, scores, MASKED)
    weights = jnp.where(allowed, jnp.exp(scores - jnp.max(scores, axis=2, keepdims=True)), 0.0)
    row_sum = jnp.sum(weights, axis=2)
    weighted = jnp.einsum(
        "qhk,khd->qhd", weights.astype(jnp.bfloat16), value_block, preferred_element_type=jnp.float32
    )
    return (weighted / row_sum[:, :, None]).astype(jnp.bfloat16).reshape(row_count, head_count * HD)


def gathered_device(hidden_in, queries, kv_prev, norm_gain, w_kv, w_out):
    row_count, local_width = queries.shape
    head_count = local_width // HD
    row_start = lax.axis_index("ctx") * row_count
    column_start = lax.axis_index("head") * local_width
    out_rows = lax.all_gather(w_out, "ctx", axis=1, tiled=True)
    kv_weights = w_kv.reshape(w_kv.shape[0], 2 * local_width)
    gain_all = norm_gain.astype(jnp.float32)
    query_heads = queries.reshape(row_count, head_count, HD)
    input_all = lax.all_gather(hidden_in, "head", axis=1, tiled=True).astype(jnp.float32)
    key_value = kv_prev
    for _ in range(ITERS):
        attended = attend_gathered(query_heads, key_value, row_start)
        partial_value = jnp.dot(attended, out_rows, preferred_element_type=jnp.float32)
        branch_sum = lax.psum(partial_value.astype(jnp.bfloat16), "head").astype(jnp.float32)
        hidden = input_all + branch_sum
        mean_square = jnp.mean(hidden * hidden, axis=1, keepdims=True)
        normed = (hidden * lax.rsqrt(mean_square + EPSILON) * gain_all).astype(jnp.bfloat16)
        fresh_kv = jnp.dot(normed, kv_weights, preferred_element_type=jnp.float32)
        hidden_out = lax.dynamic_slice_in_dim(hidden, column_start, local_width, 1)
        kv_product = fresh_kv.reshape(row_count, 2, local_width)
        key_value = kv_product.astype(jnp.bfloat16)
    return (hidden_out, kv_product)


def per_device(n, zn, *args):
    rows, width = args[1].shape
    if width == n * HD and n % CORES == 0 and rows % (16 * zn) == 0 and zn > 1:
        return fused_device(n, zn, *args)
    return gathered_device(*args)


def solution(mesh):
    in_specs = (
        P("ctx", "head"),
        P("ctx", "head"),
        P("ctx", None, "head"),
        P(),
        P(None, None, "head"),
        P("head", "ctx"),
    )
    out_specs = (P("ctx", "head"), P("ctx", None, "head"))
    return jax.shard_map(
        functools.partial(per_device, mesh.shape["ctx"], mesh.shape["head"]),
        mesh=mesh, in_specs=in_specs, out_specs=out_specs, check_vma=False,
    )
```
